32 devices in a mesh: groups: 2 (over y), exp: 4 (over z), patch: 2 (over x), band: 2 (over core).
Axes of the slice: x: 2, y: 2, z: 4, core: 2. Of those that a mesh axis runs over, the one named last changes fastest.
Arguments:
- templates: bfloat16 [8, 8, 256, 256], P(('groups', 'exp'), 'patch', None, 'band'), parts along dimension 0, may hold values from -6 to 6
- exposures: bfloat16 [8, 4, 4, 256, 256], P(('groups', 'exp'), 'patch', None, None, 'band'), parts along dimension 0, may hold values from -6 to 6
- variance: float32 [8, 4, 4, 256, 256], P(('groups', 'exp'), 'patch', None, None, 'band'), parts along dimension 0, may hold values from 0.5 to 4
- coefficients: float32 [8, 4, 4, 27], P(('groups', 'exp'), 'patch'), parts along dimension 0, may hold values from -1.2 to 1.2
- psf_width: float32 [8, 4, 4, 2], P(('groups', 'exp'), 'patch'), parts along dimension 0, may hold values from 1 to 2.5
- patch_ids: int32 [8, 4, 4], P(('groups', 'exp'), 'patch'), parts along dimension 0, may hold values from 0 to 23
- live_count: int32 [8, 4], P(('groups', 'exp'), 'patch'), parts along dimension 0, may hold values from 1 to 4
Outputs:
- coadd_diff: float32 [8, 8, 256, 256], P(('groups', 'exp'), 'patch', None, 'band'), parts along dimension 0
- score: float32 [8, 4, 4, 256, 256], P(('groups', 'exp'), 'patch', None, None, 'band'), parts along dimension 0
The draws below stay inside these ranges and needn't reach their ends.
There are 2 independent parts, one for each index of `groups`. The reference program is written for one: setup_inputs(seed, part) draws one part's arguments, and reference() takes and returns one part's arrays. A program takes and returns all parts, laid end to end along the dimension named above; each array names one. Nothing has to cross between parts.
Inputs may be any that keep to these rules, and one draw needn't show every extreme that they name: `patch_ids`: an id names patch id % 8 of the grid row id // 8 - 1 relative to the exposure's own row. `live_count`: sub-tiles at slots below the count are live.
All inputs are finite; a program needn't handle non-finite values.
Results may differ from the reference program's by a relative error of at most 0.0049.
Values may be sent and summed in bfloat16 or wider, within the bound.
A program may use at most 64 MiB of HBM per device.

```python
import math
import jax
import jax.numpy as jnp
import numpy as np
from jax import lax

S = 256
K = 4
NB = 27
HW = 10
PW = 7
NX = 4
NP = 8
NE = 4


def set_ends(entries, own_key, least, high):
    spot = [jax.random.randint(jax.random.fold_in(own_key, axis), (), 0, length) for axis, length in enumerate(entries.shape)]
    main_axis = entries.shape.index(max(entries.shape))
    neighbour = spot[:main_axis] + [(spot[main_axis] + 1) % entries.shape[main_axis]] + spot[main_axis + 1:]
    return entries.at[tuple(spot)].set(least).at[tuple(neighbour)].set(high)


def steps_of(stream_key, dims, shards, smallest, high):
    factor_of = 1.0
    for position, shards_of in shards:
        draws = jax.random.uniform(jax.random.fold_in(jax.random.fold_in(stream_key, 6), position), (shards_of,), jnp.float32, smallest / len(shards), high / len(shards))
        factor_of = factor_of * jnp.repeat(jnp.exp(draws), dims[position] // shards_of).reshape((-1,) + (1,) * (len(dims) - 1 - position))
    return factor_of


def bell_draw(own_key, extent, scale, most, pieces=(), kind=jnp.bfloat16):
    level = steps_of(own_key, extent, pieces, -0.22, 0.18) if pieces else 1.0
    values = jax.random.normal(own_key, extent, jnp.float32) * scale * level
    return jnp.minimum(jnp.maximum(values, -most), most).astype(kind)


def setup_inputs(seed: int = 0, part: int = 0) -> dict:
    streams_of = jax.random.split(jax.random.key(seed), 8)
    part_keys = jax.random.split(jax.random.fold_in(streams_of[7], part), 8)
    templates = bell_draw(part_keys[0], (NX, NP, S, S), 1.0, 6.0, ((0, 4), (1, 2), (3, 2)))
    exposures = bell_draw(part_keys[1], (NX, NE, K, S, S), 1.0, 6.0, ((0, 4), (1, 2), (4, 2)))
    variance = jnp.clip(jnp.exp(math.log(4.0) - 2.0794415 * jax.random.uniform(part_keys[2], (NX, NE, K, S, S), jnp.float32) ** steps_of(part_keys[2], (NX, NE, K, S, S), ((0, 4), (1, 2), (4, 2)), -0.2, 0.2)), 0.5, 4.0)
    coefficients = bell_draw(part_keys[3], (NX, NE, K, NB), 0.2, 1.2, ((0, 4), (1, 2)), jnp.float32)
    psf_width = jnp.clip(jnp.exp(math.log(2.5) - 0.916290732 * jax.random.uniform(part_keys[4], (NX, NE, K, 2), jnp.float32) ** steps_of(part_keys[4], (NX, NE, K, 2), ((0, 4), (1, 2)), -0.2, 0.2)), 1.0, 2.5)
    patch_ids = set_ends(jax.random.randint(part_keys[5], (NX, NE, K), 0, 3 * NP), jax.random.fold_in(part_keys[5], 1), 0, (3 * NP) - 1).astype(jnp.int32)
    live_count = set_ends(jax.random.randint(part_keys[6], (NX, NE), 1, K + 1), jax.random.fold_in(part_keys[6], 1), 1, K).astype(jnp.int32)
    return dict(templates=templates, exposures=exposures, variance=variance, coefficients=coefficients, psf_width=psf_width, patch_ids=patch_ids, live_count=live_count)


sigmas = (0.75, 1.5, 3.0)
degrees = (4, 2, 2)

def basis_terms():
    terms = []
    offset = 0
    for group in range(3):
        for first in range(degrees[group] + 1):
            for second in range(degrees[group] + 1 - first):
                terms.append((group, first, second, offset + first))
        offset = offset + degrees[group] + 1
    return terms

def membership():
    table = np.zeros((27, 11), np.float32)
    for index, term in enumerate(basis_terms()):
        table[index, term[3]] = 1.0
    return table

def profile(offset, sigma, power, reach):
    grid = jnp.arange(-reach, reach + 1).astype(jnp.float32)
    base = jnp.exp(-grid * grid / (2.0 * sigma * sigma)) * (grid / reach) ** power
    scale = jnp.sqrt(jnp.sum(base * base))
    spot = offset.astype(jnp.float32)
    value = jnp.exp(-spot * spot / (2.0 * sigma * sigma)) * (spot / reach) ** power / scale
    return jnp.where(jnp.abs(offset) <= reach, value, jnp.zeros_like(value))

def row_tables(count, reach):
    index = jnp.arange(count, dtype=jnp.int32)
    offset = index[:, None] - index[None, :]
    tables = []
    for group in range(3):
        for first in range(degrees[group] + 1):
            tables.append(profile(offset, sigmas[group], first, reach))
    return jnp.stack(tables).astype(jnp.bfloat16)

def column_tables(cols_in, cols_out, shift, reach):
    inner = jnp.arange(cols_in, dtype=jnp.int32)[:, None]
    outer = jnp.arange(cols_out, dtype=jnp.int32)[None, :]
    offset = outer + shift - inner
    return jnp.stack([profile(offset, sigmas[term[0]], term[2], reach) for term in basis_terms()])

def psf_table(offset, width, reach):
    grid = jnp.arange(-reach, reach + 1).astype(jnp.float32)
    total = jnp.sum(jnp.exp(-grid * grid / (2.0 * width * width)))
    spot = offset.astype(jnp.float32)
    value = jnp.exp(-spot * spot / (2.0 * width * width)) / total
    return jnp.where(jnp.abs(offset) <= reach, value, jnp.zeros_like(value))

def reference(templates, exposures, variance, coefficients, psf_width, patch_ids, live_count):
    padded = jnp.pad(templates, ((1, 1), (0, 0), (0, 0), (0, 0)))
    grid_row = jnp.arange(NX, dtype=jnp.int32)[:, None, None] + patch_ids // NP
    grid_col = patch_ids % NP
    live = (jnp.arange(K, dtype=jnp.int32)[None, None, :] < live_count[:, :, None]).astype(jnp.float32)
    chosen = padded[grid_row, grid_col].reshape(-1, S, S)
    gr_flat = row_tables(S, HW).reshape(-1, S)
    col_tab = column_tables(S, S, 0, HW)
    member = jnp.asarray(membership())
    index = jnp.arange(S, dtype=jnp.int32)
    offset_rows = index[:, None] - index[None, :]
    offset_cols = index[None, :] - index[:, None]

    def slot_work(items):
        template, exposure, var_tile, coeff, width, alive = items
        rows = jnp.dot(gr_flat, template, preferred_element_type=jnp.float32).astype(jnp.bfloat16).reshape(11, S, S)
        mixing = coeff[:, None] * member
        mats = jnp.einsum('kp,kcd->pcd', mixing, col_tab, precision=lax.Precision.HIGHEST).astype(jnp.bfloat16)
        convolved = jnp.einsum('psc,pcd->sd', rows.astype(jnp.float32), mats.astype(jnp.float32))
        weight = 1.0 / var_tile
        weighted = (exposure.astype(jnp.float32) - convolved) * weight
        prow = psf_table(offset_rows, width[0], PW)
        pcol = psf_table(offset_cols, width[1], PW)
        numer = jnp.dot(prow.astype(jnp.bfloat16), weighted.astype(jnp.bfloat16), preferred_element_type=jnp.float32).astype(jnp.bfloat16)
        numer = jnp.dot(numer, pcol.astype(jnp.bfloat16), preferred_element_type=jnp.float32)
        denom = jnp.dot((prow * prow).astype(jnp.bfloat16), weight.astype(jnp.bfloat16), preferred_element_type=jnp.float32).astype(jnp.bfloat16)
        denom = jnp.dot(denom, (pcol * pcol).astype(jnp.bfloat16), preferred_element_type=jnp.float32)
        return (alive * numer / jnp.sqrt(denom), alive * weighted)
    score, masked = lax.map(slot_work, (chosen, exposures.reshape(-1, S, S), variance.reshape(-1, S, S), coefficients.reshape(-1, NB), psf_width.reshape(-1, 2), live.reshape(-1)))
    coadd = jnp.zeros((NX + 2, NP, S, S), jnp.float32).at[grid_row.reshape(-1), grid_col.reshape(-1)].add(masked)
    return (coadd[1:-1], score.reshape(NX, NE, K, S, S))
```

```python
import functools

import jax
import jax.numpy as jnp
import numpy as np
from jax import lax
from jax.experimental import pallas as pl
from jax.experimental.pallas import tpu as pltpu
from jax.sharding import PartitionSpec as P

HW = 10
PW = 7

sigmas = (0.75, 1.5, 3.0)
degrees = (4, 2, 2)
starts = (0, 5, 8)
profiles = [(group, power) for group in range(3) for power in range(degrees[group] + 1)]

MESH = pl.DeviceIdType.MESH


def scale_of(group, power):
    grid = np.arange(-HW, HW + 1).astype(np.float64)
    base = np.exp(-grid * grid / (2.0 * sigmas[group] ** 2)) * (grid / HW) ** power
    return float(1.0 / np.sqrt(np.sum(base * base)))


def profile_tables(offset):
    spot = offset.astype(jnp.float32)
    inside = jnp.abs(offset) <= HW
    ratio = spot * (1.0 / HW)
    tables = []
    for group in range(3):
        value = jnp.exp(spot * spot * (-0.5 / sigmas[group] ** 2))
        value = jnp.where(inside, value, 0.0)
        for power in range(degrees[group] + 1):
            tables.append(value * scale_of(group, power))
            value = value * ratio
    return tables


def point_table(offset, width):
    rate = -0.5 / (width * width)
    total = 1.0 + 2.0 * sum(jnp.exp(rate * float(u * u)) for u in range(1, PW + 1))
    spot = offset.astype(jnp.float32)
    value = jnp.exp(spot * spot * rate) * (1.0 / total)
    return jnp.where(jnp.abs(offset) <= PW, value, 0.0)


def offsets(rows, cols, shift):
    row = lax.broadcasted_iota(jnp.int32, (rows, cols), 0)
    col = lax.broadcasted_iota(jnp.int32, (rows, cols), 1)
    return col - row + shift


def kernel(
    sizes,
    templates,
    exposures,
    variance,
    coeff,
    psf,
    ids,
    live,
    coadd,
    score,
    win,
    tfull,
    mats,
    gcat,
    gtab,
    cols,
    expo,
    inv,
    wval,
    wfull,
    ifull,
    rden,
    prow,
    qrow,
    pcol,
    qcol,
    psend,
    precv,
    pown,
    xsend,
    xrecv,
    total,
    local_sem,
    var_sem,
    exp_sem,
    out_sem,
    xs_sem,
    xr_sem,
    zs_sem,
    zr_sem,
    ts_sem,
    tr_sem,
    is_sem,
    ir_sem,
    ws_sem,
    wr_sem,
    ps_sem,
    pr_sem,
    ss_sem,
    sr_sem,
):
    Z, X, B = sizes
    owned, S, C = templates.shape[1:]
    slots = ids.shape[2]
    N = ids.shape[1] * slots
    row_patches = X * owned
    z = lax.axis_index("exp")
    x = lax.axis_index("patch")
    b = lax.axis_index("band")

    def column(o):
        return lax.rem(x + o, X)

    def back_column(o):
        return lax.rem(x + X - o, X)

    def other_band(o):
        return lax.rem(b + o, B)

    def back_band(o):
        return lax.rem(b + B - o, B)

    to_exists = (z > 0, z < Z - 1)
    from_exists = (z < Z - 1, z > 0)
    target = (z - 1, z + 1)
    lands = (2, 0)

    def remote(src, dst, send, recv, device):
        return pltpu.make_async_remote_copy(
            src_ref=src,
            dst_ref=dst,
            send_sem=send,
            recv_sem=recv,
            device_id=device,
            device_id_type=MESH,
        )

    barrier = pltpu.get_barrier_semaphore()
    for d in range(2):

        @pl.when(to_exists[d])
        def _():
            pl.semaphore_signal(barrier, inc=1, device_id={"exp": target[d]}, device_id_type=MESH)

    for o in range(1, X):
        pl.semaphore_signal(barrier, inc=1, device_id={"patch": column(o)}, device_id_type=MESH)
    for o in range(1, B):
        pl.semaphore_signal(barrier, inc=1, device_id={"band": other_band(o)}, device_id_type=MESH)

    def var_copy(n):
        return pltpu.make_async_copy(
            variance.at[0, n // slots, lax.rem(n, slots)], inv.at[n], var_sem.at[n]
        )

    def exp_copy(n):
        return pltpu.make_async_copy(
            exposures.at[0, n // slots, lax.rem(n, slots)], expo.at[n], exp_sem.at[n]
        )

    own_copy = pltpu.make_async_copy(
        templates.at[0], win.at[pl.ds(row_patches + x * owned, owned)], local_sem
    )

    def start_local(n, carry):
        var_copy(n).start()
        exp_copy(n).start()
        return carry

    lax.fori_loop(0, N, start_local, 0)
    own_copy.start()
    pl.semaphore_wait(
        barrier,
        (z > 0).astype(jnp.int32) + (z < Z - 1).astype(jnp.int32) + (X - 1) + (B - 1),
    )

    def x_copy(o, i):
        return remote(
            templates.at[0, i],
            win.at[row_patches + x * owned + i],
            xs_sem.at[o, i],
            xr_sem.at[o, i],
            {"patch": back_column(o)},
        )

    def z_copy(d, o, i):
        src = templates.at[0, i] if o == 0 else win.at[row_patches + column(o) * owned + i]
        return remote(
            src,
            win.at[lands[d] * row_patches + column(o) * owned + i],
            zs_sem.at[d, o, i],
            zr_sem.at[d, o, i],
            {"exp": target[d]},
        )

    for i in range(owned):
        for o in range(1, X):
            x_copy(o, i).start()
        for d in range(2):

            @pl.when(to_exists[d])
            def _():
                z_copy(d, 0, i).start()

    for d in range(2):

        @pl.when(jnp.logical_not(from_exists[d]))
        def _():
            for i in range(row_patches):
                win[lands[d] * row_patches + i] = jnp.zeros((S, C), jnp.bfloat16)

    def half_copy(buffer, send, recv, o, n):
        return remote(
            buffer.at[n, :, 0:C],
            buffer.at[n, :, o * C : (o + 1) * C],
            send.at[o, n],
            recv.at[o, n],
            {"band": back_band(o)},
        )

    def invert(n, carry):
        var_copy(n).wait()
        weight = 1.0 / inv[n]
        inv[n] = weight
        ifull[n, :, 0:C] = weight.astype(jnp.bfloat16)
        for o in range(1, B):
            half_copy(ifull, is_sem, ir_sem, o, n).start()
        return carry

    lax.fori_loop(0, N, invert, 0)

    for p, table in enumerate(profile_tables(-offsets(S, S, 0))):
        gcat[:, p * S : (p + 1) * S] = table.astype(jnp.bfloat16)
    shifts = [(b - other_band(o)) * C for o in range(B)]
    for o in range(B):
        for p, table in enumerate(profile_tables(offsets(C, C, shifts[o]))):
            gtab[p, o * C : (o + 1) * C, :] = table

    def forward(o, i):
        x_copy(o, i).wait_recv()
        for d in range(2):

            @pl.when(to_exists[d])
            def _():
                z_copy(d, o, i).start()

    for i in range(owned):
        for o in range(1, X):
            forward(o, i)

    def mix(n, carry):
        e, k = n // slots, lax.rem(n, slots)
        index = 0
        for p, (group, power) in enumerate(profiles):
            value = jnp.zeros((B * C, C), jnp.float32)
            for j in range(degrees[group] + 1 - power):
                value = value + coeff[0, e, k, index] * gtab[starts[group] + j]
                index += 1
            mats[n, :, p * C : (p + 1) * C] = value.astype(jnp.bfloat16)
        return carry

    lax.fori_loop(0, N, mix, 0)

    def spread(n, carry):
        e, k = n // slots, lax.rem(n, slots)
        table = point_table(offsets(S, S, 0), jnp.full((1, S), psf[0, e, k, 0], jnp.float32))
        prow[n] = table.astype(jnp.bfloat16)
        qrow[n] = (table * table).astype(jnp.bfloat16)
        width = jnp.full((1, C), psf[0, e, k, 1], jnp.float32)
        for o in range(B):
            table = point_table(offsets(C, C, shifts[o]), width)
            pcol[n, o * C : (o + 1) * C, :] = table.astype(jnp.bfloat16)
            qcol[n, o * C : (o + 1) * C, :] = (table * table).astype(jnp.bfloat16)
        return carry

    lax.fori_loop(0, N, spread, 0)

    def matched(rows, full, columns):
        middle = jnp.dot(rows, full, preferred_element_type=jnp.float32).astype(jnp.bfloat16)
        return jnp.dot(middle, columns, preferred_element_type=jnp.float32)

    def alive_of(n):
        e, k = n // slots, lax.rem(n, slots)
        return jnp.where(k < live[0, e], 1.0, 0.0).astype(jnp.float32)

    def denominator(n, carry):
        for o in range(1, B):
            half_copy(ifull, is_sem, ir_sem, o, n).wait_recv()
        rden[n] = lax.rsqrt(matched(qrow[n], ifull[n], qcol[n])) * alive_of(n)
        return carry

    lax.fori_loop(0, N, denominator, 0)

    own_copy.wait()
    for d in range(2):

        @pl.when(from_exists[d])
        def _():
            for o in range(X):
                for i in range(owned):
                    z_copy(d, o, i).wait_recv()

    def choose(n, carry):
        exp_copy(n).wait()
        tfull[n, :, 0:C] = win[ids[0, n // slots, lax.rem(n, slots)]]
        for o in range(1, B):
            half_copy(tfull, ts_sem, tr_sem, o, n).start()
        return carry

    lax.fori_loop(0, N, choose, 0)

    count = len(profiles)

    def convolve(pair, carry):
        for h in range(2):
            n = pair * 2 + h
            for o in range(1, B):
                half_copy(tfull, ts_sem, tr_sem, o, n).wait_recv()
            tile = tfull[n]
            for p in range(0, count, 2):
                wide = min(2, count - p)
                part = jnp.dot(
                    tile,
                    mats[n, :, p * C : (p + wide) * C],
                    preferred_element_type=jnp.float32,
                ).astype(jnp.bfloat16)
                for a in range(wide):
                    cols[(p + a) * S : (p + a + 1) * S, h * C : (h + 1) * C] = part[
                        :, a * C : (a + 1) * C
                    ]
        convolved = jnp.dot(gcat[...], cols[...], preferred_element_type=jnp.float32)
        for h in range(2):
            n = pair * 2 + h
            value = (expo[n].astype(jnp.float32) - convolved[:, h * C : (h + 1) * C]) * inv[n]
            wval[n] = value
            wfull[n, :, 0:C] = value.astype(jnp.bfloat16)
            for o in range(1, B):
                half_copy(wfull, ws_sem, wr_sem, o, n).start()
        return carry

    lax.fori_loop(0, N // 2, convolve, 0)

    def partial(patch):
        value = jnp.zeros((S, C), jnp.float32)
        for n in range(N):
            e, k = n // slots, n % slots
            hit = jnp.logical_and(ids[0, e, k] == patch, k < live[0, e])
            value = value + jnp.where(hit, 1.0, 0.0).astype(jnp.float32) * wval[n]
        return value

    def p_copy(d, q, t):
        return remote(
            psend.at[d, q], precv.at[d, q], ps_sem.at[d, t], pr_sem.at[d, t], {"exp": target[d]}
        )

    def patch_of(t):
        return lax.rem(x + 1 + t // owned, X) * owned + lax.rem(t, owned)

    def push(t, carry):
        q = patch_of(t)
        for d, source in ((0, 0), (1, 2)):

            @pl.when(to_exists[d])
            def _():
                psend[d, q] = partial(source * row_patches + q).astype(jnp.bfloat16)
                p_copy(d, q, t).start()

        return carry

    lax.fori_loop(0, row_patches, push, 0)

    def keep(t, carry):
        q = patch_of(t)
        pown[q] = partial(row_patches + q)
        return carry

    lax.fori_loop(0, row_patches, keep, 0)

    def out_copy(n):
        return pltpu.make_async_copy(
            rden.at[n], score.at[0, n // slots, lax.rem(n, slots)], out_sem.at[n]
        )

    def numerator(n, carry):
        for o in range(1, B):
            half_copy(wfull, ws_sem, wr_sem, o, n).wait_recv()
        rden[n] = matched(prow[n], wfull[n], pcol[n]) * rden[n]
        out_copy(n).start()
        return carry

    lax.fori_loop(0, N, numerator, 0)

    def gather_rows(t, q):
        for d in range(2):

            @pl.when(from_exists[d])
            def _():
                p_copy(d, q, t).wait_recv()
                pown[q] = pown[q] + precv[d, q].astype(jnp.float32)

    def s_copy(s, i):
        return remote(
            xsend.at[s, i],
            xrecv.at[s, i],
            ss_sem.at[s, i],
            sr_sem.at[s, i],
            {"patch": column(s + 1)},
        )

    for s in range(X - 1):
        for i in range(owned):
            t = s * owned + i
            q = column(s + 1) * owned + i
            gather_rows(t, q)
            xsend[s, i] = pown[q].astype(jnp.bfloat16)
            s_copy(s, i).start()

    final = []
    for i in range(owned):
        q = x * owned + i
        gather_rows((X - 1) * owned + i, q)
        value = pown[q]
        for s in range(X - 1):
            s_copy(s, i).wait_recv()
            value = value + xrecv[s, i].astype(jnp.float32)
        total[i] = value
        copy = pltpu.make_async_copy(total.at[i], coadd.at[0, i], out_sem.at[N + i])
        copy.start()
        final.append(copy)

    for o in range(1, X):
        for i in range(owned):
            x_copy(o, i).wait_send()
            s_copy(o - 1, i).wait_send()
    for d in range(2):

        @pl.when(to_exists[d])
        def _():
            for o in range(X):
                for i in range(owned):
                    z_copy(d, o, i).wait_send()
            for t in range(row_patches):
                p_copy(d, patch_of(t), t).wait_send()

    def finish(n, carry):
        for o in range(1, B):
            half_copy(ifull, is_sem, ir_sem, o, n).wait_send()
            half_copy(tfull, ts_sem, tr_sem, o, n).wait_send()
            half_copy(wfull, ws_sem, wr_sem, o, n).wait_send()
        out_copy(n).wait()
        return carry

    lax.fori_loop(0, N, finish, 0)
    for copy in final:
        copy.wait()


def on_device(templates, exposures, variance, coefficients, psf_width, patch_ids, live_count):
    owned, S, C = templates.shape[1:]
    Z, X, B = (lax.axis_size(axis) for axis in ("exp", "patch", "band"))
    N = patch_ids.shape[1] * patch_ids.shape[2]
    row = X * owned
    count = len(profiles)
    bf16, f32 = jnp.bfloat16, jnp.float32
    dma = pltpu.SemaphoreType.DMA
    scratch = [
        pltpu.VMEM((3 * row, S, C), bf16),
        pltpu.VMEM((N, S, B * C), bf16),
        pltpu.VMEM((N, B * C, count * C), bf16),
        pltpu.VMEM((S, count * S), bf16),
        pltpu.VMEM((count, B * C, C), f32),
        pltpu.VMEM((count * S, 2 * C), bf16),
        pltpu.VMEM((N, S, C), bf16),
        pltpu.VMEM((N, S, C), f32),
        pltpu.VMEM((N, S, C), f32),
        pltpu.VMEM((N, S, B * C), bf16),
        pltpu.VMEM((N, S, B * C), bf16),
        pltpu.VMEM((N, S, C), f32),
        pltpu.VMEM((N, S, S), bf16),
        pltpu.VMEM((N, S, S), bf16),
        pltpu.VMEM((N, B * C, C), bf16),
        pltpu.VMEM((N, B * C, C), bf16),
        pltpu.VMEM((2, row, S, C), bf16),
        pltpu.VMEM((2, row, S, C), bf16),
        pltpu.VMEM((row, S, C), f32),
        pltpu.VMEM((max(X - 1, 1), owned, S, C), bf16),
        pltpu.VMEM((max(X - 1, 1), owned, S, C), bf16),
        pltpu.VMEM((owned, S, C), f32),
        dma,
        dma((N,)),
        dma((N,)),
        dma((N + owned,)),
        dma((X, owned)),
        dma((X, owned)),
        dma((2, X, owned)),
        dma((2, X, owned)),
        dma((B, N)),
        dma((B, N)),
        dma((B, N)),
        dma((B, N)),
        dma((B, N)),
        dma((B, N)),
        dma((2, row)),
        dma((2, row)),
        dma((max(X - 1, 1), owned)),
        dma((max(X - 1, 1), owned)),
    ]
    any_spec = pl.BlockSpec(memory_space=pl.ANY)
    smem = pl.BlockSpec(memory_space=pltpu.SMEM)
    return pl.pallas_call(
        functools.partial(kernel, (Z, X, B)),
        out_shape=(
            jax.ShapeDtypeStruct(templates.shape, f32),
            jax.ShapeDtypeStruct(exposures.shape, f32),
        ),
        in_specs=[any_spec] * 3 + [smem] * 4,
        out_specs=(any_spec, any_spec),
        scratch_shapes=scratch,
        compiler_params=pltpu.CompilerParams(
            collective_id=0, has_side_effects=True, vmem_limit_bytes=56 * 2**20
        ),
    )(templates, exposures, variance, coefficients, psf_width, patch_ids, live_count)


def solution(mesh):
    in_specs = (
        P(("groups", "exp"), "patch", None, "band"),
        P(("groups", "exp"), "patch", None, None, "band"),
        P(("groups", "exp"), "patch", None, None, "band"),
        P(("groups", "exp"), "patch", None, None),
        P(("groups", "exp"), "patch", None, None),
        P(("groups", "exp"), "patch", None),
        P(("groups", "exp"), "patch"),
    )
    out_specs = (
        P(("groups", "exp"), "patch", None, "band"),
        P(("groups", "exp"), "patch", None, None, "band"),
    )
    return jax.shard_map(
        on_device, mesh=mesh, in_specs=in_specs, out_specs=out_specs, check_vma=False
    )
```

```python
import functools

import jax
import jax.numpy as jnp
import numpy as np
from jax import lax
from jax.experimental import pallas as pl
from jax.experimental.pallas import tpu as pltpu
from jax.sharding import PartitionSpec as P

HW = 10
PW = 7

sigmas = (0.75, 1.5, 3.0)
degrees = (4, 2, 2)
starts = (0, 5, 8)
profiles = [(group, power) for group in range(3) for power in range(degrees[group] + 1)]

MESH = pl.DeviceIdType.MESH


def scale_of(group, power):
    grid = np.arange(-HW, HW + 1).astype(np.float64)
    base = np.exp(-grid * grid / (2.0 * sigmas[group] ** 2)) * (grid / HW) ** power
    return float(1.0 / np.sqrt(np.sum(base * base)))


def profile_tables(offset):
    spot = offset.astype(jnp.float32)
    inside = jnp.abs(offset) <= HW
    ratio = spot * (1.0 / HW)
    tables = []
    for group in range(3):
        value = jnp.exp(spot * spot * (-0.5 / sigmas[group] ** 2))
        value = jnp.where(inside, value, 0.0)
        for power in range(degrees[group] + 1):
            tables.append(value * scale_of(group, power))
            value = value * ratio
    return tables


def point_table(offset, width):
    rate = -0.5 / (width * width)
    total = 1.0 + 2.0 * sum(jnp.exp(rate * float(u * u)) for u in range(1, PW + 1))
    spot = offset.astype(jnp.float32)
    value = jnp.exp(spot * spot * rate) * (1.0 / total)
    return jnp.where(jnp.abs(offset) <= PW, value, 0.0)


def offsets(rows, cols, shift):
    row = lax.broadcasted_iota(jnp.int32, (rows, cols), 0)
    col = lax.broadcasted_iota(jnp.int32, (rows, cols), 1)
    return col - row + shift


def kernel(
    sizes,
    templates,
    exposures,
    variance,
    coeff,
    psf,
    ids,
    live,
    coadd,
    score,
    win0,
    win1,
    tfull,
    mats,
    gcat,
    gtab,
    cols,
    expo,
    inv,
    wval,
    wfull,
    ifull,
    rden,
    prow,
    qrow,
    pcol,
    qcol,
    psend,
    precv,
    pown,
    xsend,
    xrecv,
    total,
    local_sem,
    var_sem,
    exp_sem,
    out_sem,
    xs_sem,
    xr_sem,
    zs_sem,
    zr_sem,
    ts_sem,
    tr_sem,
    is_sem,
    ir_sem,
    ws_sem,
    wr_sem,
    ps_sem,
    pr_sem,
    ss_sem,
    sr_sem,
):
    Z, X, B = sizes
    owned, S, C = templates.shape[1:]
    slots = ids.shape[2]
    N = ids.shape[1] * slots
    row_patches = X * owned
    z = lax.axis_index("exp")
    x = lax.axis_index("patch")
    b = lax.axis_index("band")

    def column(o):
        return lax.rem(x + o, X)

    def back_column(o):
        return lax.rem(x + X - o, X)

    def other_band(o):
        return lax.rem(b + o, B)

    def back_band(o):
        return lax.rem(b + B - o, B)

    to_exists = (z > 0, z < Z - 1)
    from_exists = (z < Z - 1, z > 0)
    target = (z - 1, z + 1)
    lands = (2, 0)

    def remote(src, dst, send, recv, device):
        return pltpu.make_async_remote_copy(
            src_ref=src,
            dst_ref=dst,
            send_sem=send,
            recv_sem=recv,
            device_id=device,
            device_id_type=MESH,
        )

    barrier = pltpu.get_barrier_semaphore()
    for d in range(2):

        @pl.when(to_exists[d])
        def _():
            pl.semaphore_signal(barrier, inc=1, device_id={"exp": target[d]}, device_id_type=MESH)

    for o in range(1, X):
        pl.semaphore_signal(barrier, inc=1, device_id={"patch": column(o)}, device_id_type=MESH)
    for o in range(1, B):
        pl.semaphore_signal(barrier, inc=1, device_id={"band": other_band(o)}, device_id_type=MESH)

    H = S // 2
    win = (win0, win1)
    gs = max(owned // 2, 1)
    groups = owned // gs
    bounds = ((0, H - 16), (H - 16, S))

    def var_copy(n):
        return pltpu.make_async_copy(
            variance.at[0, n // slots, lax.rem(n, slots)], inv.at[n], var_sem.at[n]
        )

    def exp_copy(n):
        return pltpu.make_async_copy(
            exposures.at[0, n // slots, lax.rem(n, slots)], expo.at[n], exp_sem.at[n]
        )

    def own_copy(h):
        return pltpu.make_async_copy(
            templates.at[0, :, pl.ds(h * H, H)],
            win[h].at[pl.ds(row_patches + x * owned, owned)],
            local_sem.at[h],
        )

    def start_local(n, carry):
        var_copy(n).start()
        return carry

    lax.fori_loop(0, N, start_local, 0)
    pl.semaphore_wait(
        barrier,
        (z > 0).astype(jnp.int32) + (z < Z - 1).astype(jnp.int32) + (X - 1) + (B - 1),
    )

    def block(h, i):
        return templates.at[0, pl.ds(i * gs, gs), pl.ds(h * H, H)]

    def place(h, row, o, i):
        return win[h].at[pl.ds(row * row_patches + column(o) * owned + i * gs, gs)]

    def x_copy(h, o, i):
        return remote(
            block(h, i),
            place(h, 1, 0, i),
            xs_sem.at[h, o, i],
            xr_sem.at[h, o, i],
            {"patch": back_column(o)},
        )

    def z_copy(h, d, o, i):
        return remote(
            block(h, i) if o == 0 else place(h, 1, o, i),
            place(h, lands[d], o, i),
            zs_sem.at[h, d, o, i],
            zr_sem.at[h, d, o, i],
            {"exp": target[d]},
        )

    def launch(h):
        for i in range(groups):
            for o in range(1, X):
                x_copy(h, o, i).start()
            for d in range(2):

                @pl.when(to_exists[d])
                def _():
                    z_copy(h, d, 0, i).start()

    def forward(h):
        for i in range(groups):
            for o in range(1, X):
                x_copy(h, o, i).wait_recv()
                for d in range(2):

                    @pl.when(to_exists[d])
                    def _():
                        z_copy(h, d, o, i).start()

    def half_copy(buffer, send, recv, o, n):
        return remote(
            buffer.at[n, :, 0:C],
            buffer.at[n, :, o * C : (o + 1) * C],
            send.at[o, n],
            recv.at[o, n],
            {"band": back_band(o)},
        )

    def invert(n, carry):
        var_copy(n).wait()
        weight = 1.0 / inv[n]
        inv[n] = weight
        ifull[n, :, 0:C] = weight.astype(jnp.bfloat16)
        for o in range(1, B):
            half_copy(ifull, is_sem, ir_sem, o, n).start()
        return carry

    launch(0)

    def start_exposure(n, carry):
        exp_copy(n).start()
        return carry

    lax.fori_loop(0, N, start_exposure, 0)
    for h in range(2):
        own_copy(h).start()
    lax.fori_loop(0, N // 2, invert, 0)
    forward(0)
    launch(1)
    lax.fori_loop(N // 2, N, invert, 0)

    count = len(profiles)
    gcat[...] = jnp.zeros((S, 2 * count * H), jnp.bfloat16)
    for p, table in enumerate(profile_tables(-offsets(H, H, 0))):
        table = table.astype(jnp.bfloat16)
        gcat[0:H, p * H : (p + 1) * H] = table
        gcat[H:S, (count + p) * H : (count + p + 1) * H] = table
    for p, table in enumerate(profile_tables(-offsets(16, H, -H))):
        gcat[H : H + 16, p * H : (p + 1) * H] = table.astype(jnp.bfloat16)
    for p, table in enumerate(profile_tables(-offsets(16, H, 16))):
        gcat[H - 16 : H, (count + p) * H : (count + p + 1) * H] = table.astype(jnp.bfloat16)
    shifts = [(b - other_band(o)) * C for o in range(B)]
    for p, table in enumerate(profile_tables(offsets(C, C, 0))):
        gtab[p, 0:C, :] = table
    for o in range(1, B):
        start = C + (o - 1) * 32
        for p, table in enumerate(profile_tables(offsets(16, C, shifts[o]))):
            gtab[p, start : start + 16, :] = table
        for p, table in enumerate(profile_tables(offsets(16, C, shifts[o] - C + 16))):
            gtab[p, start + 16 : start + 32, :] = table

    def mix(n, carry):
        e, k = n // slots, lax.rem(n, slots)
        if B > 1:
            mats[n, C : B * C, :] = jnp.zeros(((B - 1) * C, count * C), jnp.bfloat16)
        index = 0
        for p, (group, power) in enumerate(profiles):
            value = coeff[0, e, k, index] * gtab[starts[group]]
            index += 1
            for j in range(1, degrees[group] + 1 - power):
                value = value + coeff[0, e, k, index] * gtab[starts[group] + j]
                index += 1
            value = value.astype(jnp.bfloat16)
            lanes = slice(p * C, (p + 1) * C)
            mats[n, 0:C, lanes] = value[0:C]
            for o in range(1, B):
                start = C + (o - 1) * 32
                mats[n, o * C : o * C + 16, lanes] = value[start : start + 16]
                mats[n, (o + 1) * C - 16 : (o + 1) * C, lanes] = value[start + 16 : start + 32]
        return carry

    lax.fori_loop(0, N, mix, 0)
    forward(1)

    for d in range(2):

        @pl.when(jnp.logical_not(from_exists[d]))
        def _():
            for h in range(2):

                def clear(i, carry):
                    win[h][lands[d] * row_patches + i] = jnp.zeros((H, C), jnp.bfloat16)
                    return carry

                lax.fori_loop(0, row_patches, clear, 0)

    def spread(n, carry):
        e, k = n // slots, lax.rem(n, slots)

        def put(low, square, rows, lanes, table):
            low[n, rows, lanes] = table.astype(jnp.bfloat16)
            square[n, rows, lanes] = (table * table).astype(jnp.bfloat16)

        width = jnp.full((1, H), psf[0, e, 0, k], jnp.float32)
        prow[n] = jnp.zeros((S, S), jnp.bfloat16)
        qrow[n] = jnp.zeros((S, S), jnp.bfloat16)
        table = point_table(offsets(H, H, 0), width)
        put(prow, qrow, slice(0, H), slice(0, H), table)
        put(prow, qrow, slice(H, S), slice(H, S), table)
        put(prow, qrow, slice(H, H + 16), slice(0, H), point_table(offsets(16, H, -H), width))
        put(prow, qrow, slice(H - 16, H), slice(H, S), point_table(offsets(16, H, 16), width))
        width = jnp.full((1, C), psf[0, e, 1, k], jnp.float32)
        pcol[n] = jnp.zeros((B * C, C), jnp.bfloat16)
        qcol[n] = jnp.zeros((B * C, C), jnp.bfloat16)
        lanes = slice(0, C)
        put(pcol, qcol, slice(0, C), lanes, point_table(offsets(C, C, 0), width))
        for o in range(1, B):
            first, last = o * C, (o + 1) * C
            table = point_table(offsets(16, C, shifts[o]), width)
            put(pcol, qcol, slice(first, first + 16), lanes, table)
            table = point_table(offsets(16, C, shifts[o] - C + 16), width)
            put(pcol, qcol, slice(last - 16, last), lanes, table)
        return carry

    def alive_of(n):
        e, k = n // slots, lax.rem(n, slots)
        return jnp.where(k < live[0, e], 1.0, 0.0).astype(jnp.float32)

    def matched(chains):
        middle = [
            jnp.dot(rows, full, preferred_element_type=jnp.float32).astype(jnp.bfloat16)
            for rows, full, _ in chains
        ]
        return [
            jnp.dot(part, chain[2], preferred_element_type=jnp.float32)
            for part, chain in zip(middle, chains)
        ]

    def denominator(pair, carry):
        tiles = (pair * 2, pair * 2 + 1)
        for n in tiles:
            for o in range(1, B):
                half_copy(ifull, is_sem, ir_sem, o, n).wait_recv()
        results = matched([(qrow[n], ifull[n], qcol[n]) for n in tiles])
        for n, result in zip(tiles, results):
            rden[n] = lax.rsqrt(result) * alive_of(n)
        return carry

    def arrive(h):
        own_copy(h).wait()
        for d in range(2):

            @pl.when(from_exists[d])
            def _():
                for o in range(X):
                    for i in range(groups):
                        z_copy(h, d, o, i).wait_recv()

    def tile_copy(h, o, n):
        return remote(
            tfull.at[h, n, :, 0:C],
            tfull.at[h, n, :, o * C : (o + 1) * C],
            ts_sem.at[h, o, n],
            tr_sem.at[h, o, n],
            {"band": back_band(o)},
        )

    def middle(h):
        first, last = bounds[h]
        depth = (h + 1) * count * H

        def choose(n, carry):
            tfull[h, n, :, 0:C] = win[h][ids[0, n // slots, lax.rem(n, slots)]]
            for o in range(1, B):
                tile_copy(h, o, n).start()
            return carry

        lax.fori_loop(0, N, choose, 0)

        def convolve(pair, carry):
            for a in range(2):
                n = pair * 2 + a
                if h == 0:
                    exp_copy(n).wait()
                for o in range(1, B):
                    tile_copy(h, o, n).wait_recv()
                tile = tfull[h, n]
                for p in range(0, count, 2):
                    wide = min(2, count - p)
                    part = jnp.dot(
                        tile,
                        mats[n, :, p * C : (p + wide) * C],
                        preferred_element_type=jnp.float32,
                    ).astype(jnp.bfloat16)
                    for v in range(wide):
                        row = (h * count + p + v) * H
                        cols[pair, row : row + H, a * C : (a + 1) * C] = part[
                            :, v * C : (v + 1) * C
                        ]
            convolved = jnp.dot(
                gcat[first:last, 0:depth],
                cols[pair, 0:depth, :],
                preferred_element_type=jnp.float32,
            )
            for a in range(2):
                n = pair * 2 + a
                value = expo[n, first:last, :].astype(jnp.float32)
                value = (value - convolved[:, a * C : (a + 1) * C]) * inv[n, first:last, :]
                wval[n, first:last, :] = value
                wfull[n, first:last, 0:C] = value.astype(jnp.bfloat16)
                if h == 1:
                    for o in range(1, B):
                        half_copy(wfull, ws_sem, wr_sem, o, n).start()
            return carry

        lax.fori_loop(0, N // 2, convolve, 0)

    def partial(h, patch):
        first, last = bounds[h]
        value = jnp.zeros((last - first, C), jnp.float32)
        for n in range(N):
            e, k = n // slots, n % slots
            hit = jnp.logical_and(ids[0, e, k] == patch, k < live[0, e])
            factor = jnp.where(hit, 1.0, 0.0).astype(jnp.float32)
            value = value + factor * wval[n, first:last, :]
        return value

    def p_copy(h, d, q, t):
        first, last = bounds[h]
        rows = pl.ds(first, last - first)
        return remote(
            psend.at[d, q, rows],
            precv.at[d, q, rows],
            ps_sem.at[h, d, t],
            pr_sem.at[h, d, t],
            {"exp": target[d]},
        )

    def patch_of(t):
        return lax.rem(x + 1 + t // owned, X) * owned + lax.rem(t, owned)

    def push(h):
        first, last = bounds[h]

        def step(t, carry):
            q = patch_of(t)
            for d, source in ((0, 0), (1, 2)):

                @pl.when(to_exists[d])
                def _():
                    value = partial(h, source * row_patches + q)
                    psend[d, q, first:last, :] = value.astype(jnp.bfloat16)
                    p_copy(h, d, q, t).start()

            return carry

        lax.fori_loop(0, row_patches, step, 0)

    def keep(h):
        first, last = bounds[h]

        def step(q, carry):
            pown[q, first:last, :] = partial(h, row_patches + q)
            return carry

        lax.fori_loop(0, row_patches, step, 0)

    def out_copy(n):
        return pltpu.make_async_copy(
            rden.at[n], score.at[0, n // slots, lax.rem(n, slots)], out_sem.at[n]
        )

    def numerator(pair, carry):
        tiles = (pair * 2, pair * 2 + 1)
        for n in tiles:
            for o in range(1, B):
                half_copy(wfull, ws_sem, wr_sem, o, n).wait_recv()
        results = matched([(prow[n], wfull[n], pcol[n]) for n in tiles])
        for n, result in zip(tiles, results):
            rden[n] = result * rden[n]
            out_copy(n).start()
        return carry

    def gather_rows(h, t, q):
        first, last = bounds[h]
        for d in range(2):

            @pl.when(from_exists[d])
            def _():
                p_copy(h, d, q, t).wait_recv()
                pown[q, first:last, :] += precv[d, q, first:last, :].astype(jnp.float32)

    def s_copy(h, s, i):
        first, last = bounds[h]
        rows = pl.ds(first, last - first)
        return remote(
            xsend.at[s, i, rows],
            xrecv.at[s, i, rows],
            ss_sem.at[h, s, i],
            sr_sem.at[h, s, i],
            {"patch": column(s + 1)},
        )

    def pass_on(h):
        first, last = bounds[h]
        for s in range(X - 1):
            for i in range(owned):
                q = column(s + 1) * owned + i
                gather_rows(h, s * owned + i, q)
                xsend[s, i, first:last, :] = pown[q, first:last, :].astype(jnp.bfloat16)
                s_copy(h, s, i).start()

    def final_copy(h, i):
        first, last = bounds[h]
        rows = pl.ds(first, last - first)
        return pltpu.make_async_copy(
            total.at[i, rows], coadd.at[0, i, rows], out_sem.at[N + h * owned + i]
        )

    def finish_sums(h):
        first, last = bounds[h]
        for i in range(owned):
            q = x * owned + i
            gather_rows(h, (X - 1) * owned + i, q)
            value = pown[q, first:last, :]
            for s in range(X - 1):
                s_copy(h, s, i).wait_recv()
                value = value + xrecv[s, i, first:last, :].astype(jnp.float32)
            total[i, first:last, :] = value
            final_copy(h, i).start()

    arrive(0)
    middle(0)
    push(0)
    lax.fori_loop(0, N, spread, 0)
    arrive(1)
    middle(1)
    push(1)
    keep(0)
    pass_on(0)
    keep(1)
    lax.fori_loop(0, N // 2, denominator, 0)
    pass_on(1)
    finish_sums(0)
    lax.fori_loop(0, N // 2, numerator, 0)
    finish_sums(1)

    for h in range(2):
        for o in range(1, X):
            for i in range(groups):
                x_copy(h, o, i).wait_send()
            for i in range(owned):
                s_copy(h, o - 1, i).wait_send()
        for i in range(owned):
            final_copy(h, i).wait()
        for d in range(2):

            @pl.when(to_exists[d])
            def _():
                for o in range(X):
                    for i in range(groups):
                        z_copy(h, d, o, i).wait_send()

                def sent(t, carry):
                    p_copy(h, d, patch_of(t), t).wait_send()
                    return carry

                lax.fori_loop(0, row_patches, sent, 0)

    def finish(n, carry):
        for o in range(1, B):
            half_copy(ifull, is_sem, ir_sem, o, n).wait_send()
            half_copy(wfull, ws_sem, wr_sem, o, n).wait_send()
            for h in range(2):
                tile_copy(h, o, n).wait_send()
        out_copy(n).wait()
        return carry

    lax.fori_loop(0, N, finish, 0)


def on_device(templates, exposures, variance, coefficients, psf_width, patch_ids, live_count):
    owned, S, C = templates.shape[1:]
    Z, X, B = (lax.axis_size(axis) for axis in ("exp", "patch", "band"))
    N = patch_ids.shape[1] * patch_ids.shape[2]
    row = X * owned
    count = len(profiles)
    bf16, f32 = jnp.bfloat16, jnp.float32
    dma = pltpu.SemaphoreType.DMA
    scratch = [
        pltpu.VMEM((3 * row, S // 2, C), bf16),
        pltpu.VMEM((3 * row, S // 2, C), bf16),
        pltpu.VMEM((2, N, S // 2, B * C), bf16),
        pltpu.VMEM((N, B * C, count * C), bf16),
        pltpu.VMEM((S, count * S), bf16),
        pltpu.VMEM((count, C + 32 * (B - 1), C), f32),
        pltpu.VMEM((N // 2, count * S, 2 * C), bf16),
        pltpu.VMEM((N, S, C), bf16),
        pltpu.VMEM((N, S, C), f32),
        pltpu.VMEM((N, S, C), f32),
        pltpu.VMEM((N, S, B * C), bf16),
        pltpu.VMEM((N, S, B * C), bf16),
        pltpu.VMEM((N, S, C), f32),
        pltpu.VMEM((N, S, S), bf16),
        pltpu.VMEM((N, S, S), bf16),
        pltpu.VMEM((N, B * C, C), bf16),
        pltpu.VMEM((N, B * C, C), bf16),
        pltpu.VMEM((2, row, S, C), bf16),
        pltpu.VMEM((2, row, S, C), bf16),
        pltpu.VMEM((row, S, C), f32),
        pltpu.VMEM((max(X - 1, 1), owned, S, C), bf16),
        pltpu.VMEM((max(X - 1, 1), owned, S, C), bf16),
        pltpu.VMEM((owned, S, C), f32),
        dma((2,)),
        dma((N,)),
        dma((N,)),
        dma((N + 2 * owned,)),
        dma((2, X, owned)),
        dma((2, X, owned)),
        dma((2, 2, X, owned)),
        dma((2, 2, X, owned)),
        dma((2, B, N)),
        dma((2, B, N)),
        dma((B, N)),
        dma((B, N)),
        dma((B, N)),
        dma((B, N)),
        dma((2, 2, row)),
        dma((2, 2, row)),
        dma((2, max(X - 1, 1), owned)),
        dma((2, max(X - 1, 1), owned)),
    ]
    any_spec = pl.BlockSpec(memory_space=pl.ANY)
    smem = pl.BlockSpec(memory_space=pltpu.SMEM)
    return pl.pallas_call(
        functools.partial(kernel, (Z, X, B)),
        out_shape=(
            jax.ShapeDtypeStruct(templates.shape, f32),
            jax.ShapeDtypeStruct(exposures.shape, f32),
        ),
        in_specs=[any_spec] * 3 + [smem] * 4,
        out_specs=(any_spec, any_spec),
        scratch_shapes=scratch,
        compiler_params=pltpu.CompilerParams(
            collective_id=0, has_side_effects=True, vmem_limit_bytes=56 * 2**20
        ),
    )(
        templates,
        exposures,
        variance,
        coefficients,
        jnp.swapaxes(psf_width, 2, 3),
        patch_ids,
        live_count,
    )


def solution(mesh):
    in_specs = (
        P(("groups", "exp"), "patch", None, "band"),
        P(("groups", "exp"), "patch", None, None, "band"),
        P(("groups", "exp"), "patch", None, None, "band"),
        P(("groups", "exp"), "patch", None, None),
        P(("groups", "exp"), "patch", None, None),
        P(("groups", "exp"), "patch", None),
        P(("groups", "exp"), "patch"),
    )
    out_specs = (
        P(("groups", "exp"), "patch", None, "band"),
        P(("groups", "exp"), "patch", None, None, "band"),
    )
    return jax.shard_map(
        on_device, mesh=mesh, in_specs=in_specs, out_specs=out_specs, check_vma=False
    )
```

```python
import functools

import jax
import jax.numpy as jnp
import numpy as np
from jax import lax
from jax.experimental import pallas as pl
from jax.experimental.pallas import tpu as pltpu
from jax.sharding import PartitionSpec as P

HW = 10
PW = 7

sigmas = (0.75, 1.5, 3.0)
degrees = (4, 2, 2)
starts = (0, 5, 8)
profiles = [(group, power) for group in range(3) for power in range(degrees[group] + 1)]

MESH = pl.DeviceIdType.MESH


def scale_of(group, power):
    grid = np.arange(-HW, HW + 1).astype(np.float64)
    base = np.exp(-grid * grid / (2.0 * sigmas[group] ** 2)) * (grid / HW) ** power
    return float(1.0 / np.sqrt(np.sum(base * base)))


def profile_tables(offset):
    spot = offset.astype(jnp.float32)
    inside = jnp.abs(offset) <= HW
    ratio = spot * (1.0 / HW)
    tables = []
    for group in range(3):
        value = jnp.exp(spot * spot * (-0.5 / sigmas[group] ** 2))
        value = jnp.where(inside, value, 0.0)
        for power in range(degrees[group] + 1):
            tables.append(value * scale_of(group, power))
            value = value * ratio
    return tables


def point_table(offset, width):
    rate = -0.5 / (width * width)
    total = 1.0 + 2.0 * sum(jnp.exp(rate * float(u * u)) for u in range(1, PW + 1))
    spot = offset.astype(jnp.float32)
    value = jnp.exp(spot * spot * rate) * (1.0 / total)
    return jnp.where(jnp.abs(offset) <= PW, value, 0.0)


def offsets(rows, cols, shift):
    row = lax.broadcasted_iota(jnp.int32, (rows, cols), 0)
    col = lax.broadcasted_iota(jnp.int32, (rows, cols), 1)
    return col - row + shift


def kernel(
    sizes,
    templates,
    exposures,
    variance,
    coeff,
    psf,
    ids,
    live,
    coadd,
    score,
    win0,
    win1,
    tfull,
    mats,
    gcat,
    gtab,
    cols,
    expo,
    inv,
    wval,
    wfull,
    ifull,
    rden,
    prow,
    qrow,
    pcol,
    qcol,
    psend,
    precv,
    pown,
    xsend,
    xrecv,
    local_sem,
    var_sem,
    exp_sem,
    xs_sem,
    xr_sem,
    zs_sem,
    zr_sem,
    ts_sem,
    tr_sem,
    is_sem,
    ir_sem,
    ws_sem,
    wr_sem,
    ps_sem,
    pr_sem,
    ss_sem,
    sr_sem,
):
    Z, X, B = sizes
    owned, S, C = templates.shape[1:]
    slots = ids.shape[2]
    N = ids.shape[1] * slots
    row_patches = X * owned
    z = lax.axis_index("exp")
    x = lax.axis_index("patch")
    b = lax.axis_index("band")

    def column(o):
        return lax.rem(x + o, X)

    def back_column(o):
        return lax.rem(x + X - o, X)

    def other_band(o):
        return lax.rem(b + o, B)

    def back_band(o):
        return lax.rem(b + B - o, B)

    to_exists = (z > 0, z < Z - 1)
    from_exists = (z < Z - 1, z > 0)
    target = (z - 1, z + 1)
    lands = (2, 0)

    def remote(src, dst, send, recv, device):
        return pltpu.make_async_remote_copy(
            src_ref=src,
            dst_ref=dst,
            send_sem=send,
            recv_sem=recv,
            device_id=device,
            device_id_type=MESH,
        )

    barrier = pltpu.get_barrier_semaphore()
    for d in range(2):

        @pl.when(to_exists[d])
        def _():
            pl.semaphore_signal(barrier, inc=1, device_id={"exp": target[d]}, device_id_type=MESH)

    for o in range(1, X):
        pl.semaphore_signal(barrier, inc=1, device_id={"patch": column(o)}, device_id_type=MESH)
    for o in range(1, B):
        pl.semaphore_signal(barrier, inc=1, device_id={"band": other_band(o)}, device_id_type=MESH)

    H = S // 2
    win = (win0, win1)
    gs = max(owned // 2, 1)
    groups = owned // gs
    bounds = ((0, H - 16), (H - 16, S))

    def var_copy(n):
        return pltpu.make_async_copy(
            variance.at[0, n // slots, lax.rem(n, slots)], inv.at[n], var_sem.at[n]
        )

    def exp_copy(n):
        return pltpu.make_async_copy(
            exposures.at[0, n // slots, lax.rem(n, slots)], expo.at[n], exp_sem.at[n]
        )

    def own_copy(h):
        return pltpu.make_async_copy(
            templates.at[0, :, pl.ds(h * H, H)],
            win[h].at[pl.ds(row_patches + x * owned, owned)],
            local_sem.at[h],
        )

    def start_local(n, carry):
        var_copy(n).start()
        return carry

    lax.fori_loop(0, N, start_local, 0)
    pl.semaphore_wait(
        barrier,
        (z > 0).astype(jnp.int32) + (z < Z - 1).astype(jnp.int32) + (X - 1) + (B - 1),
    )

    def block(h, i):
        return templates.at[0, pl.ds(i * gs, gs), pl.ds(h * H, H)]

    def place(h, row, o, i):
        return win[h].at[pl.ds(row * row_patches + column(o) * owned + i * gs, gs)]

    def x_copy(h, o, i):
        return remote(
            block(h, i),
            place(h, 1, 0, i),
            xs_sem.at[h, o, i],
            xr_sem.at[h, o, i],
            {"patch": back_column(o)},
        )

    def z_copy(h, d, o, i):
        return remote(
            block(h, i) if o == 0 else place(h, 1, o, i),
            place(h, lands[d], o, i),
            zs_sem.at[h, d, o, i],
            zr_sem.at[h, d, o, i],
            {"exp": target[d]},
        )

    def launch(h):
        for i in range(groups):
            for o in range(1, X):
                x_copy(h, o, i).start()
            for d in range(2):

                @pl.when(to_exists[d])
                def _():
                    z_copy(h, d, 0, i).start()

    def forward(h):
        for i in range(groups):
            for o in range(1, X):
                x_copy(h, o, i).wait_recv()
                for d in range(2):

                    @pl.when(to_exists[d])
                    def _():
                        z_copy(h, d, o, i).start()

    def half_copy(buffer, send, recv, o, n):
        return remote(
            buffer.at[n, :, 0:C],
            buffer.at[n, :, o * C : (o + 1) * C],
            send.at[o, n],
            recv.at[o, n],
            {"band": back_band(o)},
        )

    def invert(n, carry):
        var_copy(n).wait()
        weight = 1.0 / inv[n]
        inv[n] = weight
        ifull[n, :, 0:C] = weight.astype(jnp.bfloat16)
        for o in range(1, B):
            half_copy(ifull, is_sem, ir_sem, o, n).start()
        return carry

    launch(0)

    def start_exposure(n, carry):
        exp_copy(n).start()
        return carry

    lax.fori_loop(0, N, start_exposure, 0)
    for h in range(2):
        own_copy(h).start()
    lax.fori_loop(0, N // 2, invert, 0)
    forward(0)
    launch(1)
    lax.fori_loop(N // 2, N, invert, 0)

    count = len(profiles)
    gcat[...] = jnp.zeros((S, 2 * count * H), jnp.bfloat16)
    for p, table in enumerate(profile_tables(-offsets(H, H, 0))):
        table = table.astype(jnp.bfloat16)
        gcat[0:H, p * H : (p + 1) * H] = table
        gcat[H:S, (count + p) * H : (count + p + 1) * H] = table
    for p, table in enumerate(profile_tables(-offsets(16, H, -H))):
        gcat[H : H + 16, p * H : (p + 1) * H] = table.astype(jnp.bfloat16)
    for p, table in enumerate(profile_tables(-offsets(16, H, 16))):
        gcat[H - 16 : H, (count + p) * H : (count + p + 1) * H] = table.astype(jnp.bfloat16)
    shifts = [(b - other_band(o)) * C for o in range(B)]
    for p, table in enumerate(profile_tables(offsets(C, C, 0))):
        gtab[p, 0:C, :] = table
    for o in range(1, B):
        start = C + (o - 1) * 32
        for p, table in enumerate(profile_tables(offsets(16, C, shifts[o]))):
            gtab[p, start : start + 16, :] = table
        for p, table in enumerate(profile_tables(offsets(16, C, shifts[o] - C + 16))):
            gtab[p, start + 16 : start + 32, :] = table

    def mix(n, carry):
        e, k = n // slots, lax.rem(n, slots)
        if B > 1:
            mats[n, C : B * C, :] = jnp.zeros(((B - 1) * C, count * C), jnp.bfloat16)
        index = 0
        for p, (group, power) in enumerate(profiles):
            value = coeff[0, e, k, index] * gtab[starts[group]]
            index += 1
            for j in range(1, degrees[group] + 1 - power):
                value = value + coeff[0, e, k, index] * gtab[starts[group] + j]
                index += 1
            value = value.astype(jnp.bfloat16)
            lanes = slice(p * C, (p + 1) * C)
            mats[n, 0:C, lanes] = value[0:C]
            for o in range(1, B):
                start = C + (o - 1) * 32
                mats[n, o * C : o * C + 16, lanes] = value[start : start + 16]
                mats[n, (o + 1) * C - 16 : (o + 1) * C, lanes] = value[start + 16 : start + 32]
        return carry

    lax.fori_loop(0, N, mix, 0)
    forward(1)

    for d in range(2):

        @pl.when(jnp.logical_not(from_exists[d]))
        def _():
            for h in range(2):

                def clear(i, carry):
                    win[h][lands[d] * row_patches + i] = jnp.zeros((H, C), jnp.bfloat16)
                    return carry

                lax.fori_loop(0, row_patches, clear, 0)

    def spread(n, carry):
        e, k = n // slots, lax.rem(n, slots)

        def put(low, square, rows, lanes, table):
            low[n, rows, lanes] = table.astype(jnp.bfloat16)
            square[n, rows, lanes] = (table * table).astype(jnp.bfloat16)

        width = jnp.full((1, H), psf[0, e, 0, k], jnp.float32)
        prow[n] = jnp.zeros((S, S), jnp.bfloat16)
        qrow[n] = jnp.zeros((S, S), jnp.bfloat16)
        table = point_table(offsets(H, H, 0), width)
        put(prow, qrow, slice(0, H), slice(0, H), table)
        put(prow, qrow, slice(H, S), slice(H, S), table)
        put(prow, qrow, slice(H, H + 16), slice(0, H), point_table(offsets(16, H, -H), width))
        put(prow, qrow, slice(H - 16, H), slice(H, S), point_table(offsets(16, H, 16), width))
        width = jnp.full((1, C), psf[0, e, 1, k], jnp.float32)
        pcol[n] = jnp.zeros((B * C, C), jnp.bfloat16)
        qcol[n] = jnp.zeros((B * C, C), jnp.bfloat16)
        lanes = slice(0, C)
        put(pcol, qcol, slice(0, C), lanes, point_table(offsets(C, C, 0), width))
        for o in range(1, B):
            first, last = o * C, (o + 1) * C
            table = point_table(offsets(16, C, shifts[o]), width)
            put(pcol, qcol, slice(first, first + 16), lanes, table)
            table = point_table(offsets(16, C, shifts[o] - C + 16), width)
            put(pcol, qcol, slice(last - 16, last), lanes, table)
        return carry

    def alive_of(n):
        e, k = n // slots, lax.rem(n, slots)
        return jnp.where(k < live[0, e], 1.0, 0.0).astype(jnp.float32)

    def matched(chains):
        middle = [
            jnp.dot(rows, full, preferred_element_type=jnp.float32).astype(jnp.bfloat16)
            for rows, full, _ in chains
        ]
        return [
            jnp.dot(part, chain[2], preferred_element_type=jnp.float32)
            for part, chain in zip(middle, chains)
        ]

    def denominator(pair, carry):
        tiles = (pair * 2, pair * 2 + 1)
        for n in tiles:
            for o in range(1, B):
                half_copy(ifull, is_sem, ir_sem, o, n).wait_recv()
        results = matched([(qrow[n], ifull[n], qcol[n]) for n in tiles])
        for n, result in zip(tiles, results):
            rden[n] = lax.rsqrt(result) * alive_of(n)
        return carry

    def arrive(h):
        own_copy(h).wait()
        for d in range(2):

            @pl.when(from_exists[d])
            def _():
                for o in range(X):
                    for i in range(groups):
                        z_copy(h, d, o, i).wait_recv()

    def tile_copy(h, o, n):
        return remote(
            tfull.at[h, n, :, 0:C],
            tfull.at[h, n, :, o * C : (o + 1) * C],
            ts_sem.at[h, o, n],
            tr_sem.at[h, o, n],
            {"band": back_band(o)},
        )

    def middle(h):
        first, last = bounds[h]
        depth = (h + 1) * count * H

        def choose(n, carry):
            tfull[h, n, :, 0:C] = win[h][ids[0, n // slots, lax.rem(n, slots)]]
            for o in range(1, B):
                tile_copy(h, o, n).start()
            return carry

        lax.fori_loop(0, N, choose, 0)

        def convolve(pair, carry):
            for a in range(2):
                n = pair * 2 + a
                if h == 0:
                    exp_copy(n).wait()
                for o in range(1, B):
                    tile_copy(h, o, n).wait_recv()
                tile = tfull[h, n]
                for p in range(0, count, 2):
                    wide = min(2, count - p)
                    part = jnp.dot(
                        tile,
                        mats[n, :, p * C : (p + wide) * C],
                        preferred_element_type=jnp.float32,
                    ).astype(jnp.bfloat16)
                    for v in range(wide):
                        row = (h * count + p + v) * H
                        cols[pair, row : row + H, a * C : (a + 1) * C] = part[
                            :, v * C : (v + 1) * C
                        ]
            convolved = jnp.dot(
                gcat[first:last, 0:depth],
                cols[pair, 0:depth, :],
                preferred_element_type=jnp.float32,
            )
            for a in range(2):
                n = pair * 2 + a
                value = expo[n, first:last, :].astype(jnp.float32)
                value = (value - convolved[:, a * C : (a + 1) * C]) * inv[n, first:last, :]
                wval[n, first:last, :] = value
                wfull[n, first:last, 0:C] = value.astype(jnp.bfloat16)
                if h == 1:
                    for o in range(1, B):
                        half_copy(wfull, ws_sem, wr_sem, o, n).start()
            return carry

        lax.fori_loop(0, N // 2, convolve, 0)

    def partials(h, q, rows):
        first, last = bounds[h]
        factors = []
        for row in rows:
            hits = []
            for n in range(N):
                e, k = n // slots, n % slots
                hit = jnp.logical_and(ids[0, e, k] == row * row_patches + q, k < live[0, e])
                hits.append(jnp.where(hit, 1.0, 0.0).astype(jnp.float32))
            factors.append(hits)
        step = 16
        for start in range(first, last, step):
            values = [jnp.zeros((step, C), jnp.float32) for _ in rows]
            for n in range(N):
                tile = wval[n, start : start + step, :]
                values = [value + hits[n] * tile for value, hits in zip(values, factors)]
            yield slice(start, start + step), values

    def p_copy(h, d, q, t):
        first, last = bounds[h]
        rows = pl.ds(first, last - first)
        return remote(
            psend.at[d, q, rows],
            precv.at[d, q, rows],
            ps_sem.at[h, d, t],
            pr_sem.at[h, d, t],
            {"exp": target[d]},
        )

    def patch_of(t):
        return lax.rem(x + 1 + t // owned, X) * owned + lax.rem(t, owned)

    def push(h):
        def step(t, carry):
            q = patch_of(t)
            for rows, (up, own, down) in partials(h, q, (0, 1, 2)):
                psend[0, q, rows, :] = up.astype(jnp.bfloat16)
                psend[1, q, rows, :] = down.astype(jnp.bfloat16)
                pown[q, rows, :] = own
            for d in range(2):

                @pl.when(to_exists[d])
                def _():
                    p_copy(h, d, q, t).start()

            return carry

        lax.fori_loop(0, row_patches, step, 0)

    def numerator(pair, carry):
        tiles = (pair * 2, pair * 2 + 1)
        for n in tiles:
            for o in range(1, B):
                half_copy(wfull, ws_sem, wr_sem, o, n).wait_recv()
        results = matched([(prow[n], wfull[n], pcol[n]) for n in tiles])
        for n, result in zip(tiles, results):
            score[0, n // slots, lax.rem(n, slots)] = result * rden[n]
        return carry

    def gather_rows(h, t, q):
        first, last = bounds[h]
        for d in range(2):

            @pl.when(from_exists[d])
            def _():
                p_copy(h, d, q, t).wait_recv()
                pown[q, first:last, :] += precv[d, q, first:last, :].astype(jnp.float32)

    def s_copy(h, s, i):
        first, last = bounds[h]
        rows = pl.ds(first, last - first)
        return remote(
            xsend.at[s, i, rows],
            xrecv.at[s, i, rows],
            ss_sem.at[h, s, i],
            sr_sem.at[h, s, i],
            {"patch": column(s + 1)},
        )

    def pass_on(h):
        first, last = bounds[h]
        for s in range(X - 1):
            for i in range(owned):
                q = column(s + 1) * owned + i
                gather_rows(h, s * owned + i, q)
                xsend[s, i, first:last, :] = pown[q, first:last, :].astype(jnp.bfloat16)
                s_copy(h, s, i).start()

    def finish_sums(h):
        first, last = bounds[h]
        for i in range(owned):
            q = x * owned + i
            gather_rows(h, (X - 1) * owned + i, q)
            value = pown[q, first:last, :]
            for s in range(X - 1):
                s_copy(h, s, i).wait_recv()
                value = value + xrecv[s, i, first:last, :].astype(jnp.float32)
            coadd[0, i, first:last, :] = value

    arrive(0)
    middle(0)
    push(0)
    lax.fori_loop(0, N, spread, 0)
    arrive(1)
    middle(1)
    push(1)
    pass_on(0)
    lax.fori_loop(0, N // 2, denominator, 0)
    pass_on(1)
    finish_sums(0)
    lax.fori_loop(0, N // 2, numerator, 0)
    finish_sums(1)

    for h in range(2):
        for o in range(1, X):
            for i in range(groups):
                x_copy(h, o, i).wait_send()
            for i in range(owned):
                s_copy(h, o - 1, i).wait_send()
        for d in range(2):

            @pl.when(to_exists[d])
            def _():
                for o in range(X):
                    for i in range(groups):
                        z_copy(h, d, o, i).wait_send()

                def sent(t, carry):
                    p_copy(h, d, patch_of(t), t).wait_send()
                    return carry

                lax.fori_loop(0, row_patches, sent, 0)

    def finish(n, carry):
        for o in range(1, B):
            half_copy(ifull, is_sem, ir_sem, o, n).wait_send()
            half_copy(wfull, ws_sem, wr_sem, o, n).wait_send()
            for h in range(2):
                tile_copy(h, o, n).wait_send()
        return carry

    lax.fori_loop(0, N, finish, 0)


def on_device(templates, exposures, variance, coefficients, psf_width, patch_ids, live_count):
    owned, S, C = templates.shape[1:]
    Z, X, B = (lax.axis_size(axis) for axis in ("exp", "patch", "band"))
    N = patch_ids.shape[1] * patch_ids.shape[2]
    row = X * owned
    count = len(profiles)
    bf16, f32 = jnp.bfloat16, jnp.float32
    dma = pltpu.SemaphoreType.DMA
    scratch = [
        pltpu.VMEM((3 * row, S // 2, C), bf16),
        pltpu.VMEM((3 * row, S // 2, C), bf16),
        pltpu.VMEM((2, N, S // 2, B * C), bf16),
        pltpu.VMEM((N, B * C, count * C), bf16),
        pltpu.VMEM((S, count * S), bf16),
        pltpu.VMEM((count, C + 32 * (B - 1), C), f32),
        pltpu.VMEM((N // 2, count * S, 2 * C), bf16),
        pltpu.VMEM((N, S, C), bf16),
        pltpu.VMEM((N, S, C), f32),
        pltpu.VMEM((N, S, C), f32),
        pltpu.VMEM((N, S, B * C), bf16),
        pltpu.VMEM((N, S, B * C), bf16),
        pltpu.VMEM((N, S, C), f32),
        pltpu.VMEM((N, S, S), bf16),
        pltpu.VMEM((N, S, S), bf16),
        pltpu.VMEM((N, B * C, C), bf16),
        pltpu.VMEM((N, B * C, C), bf16),
        pltpu.VMEM((2, row, S, C), bf16),
        pltpu.VMEM((2, row, S, C), bf16),
        pltpu.VMEM((row, S, C), f32),
        pltpu.VMEM((max(X - 1, 1), owned, S, C), bf16),
        pltpu.VMEM((max(X - 1, 1), owned, S, C), bf16),
        dma((2,)),
        dma((N,)),
        dma((N,)),
        dma((2, X, owned)),
        dma((2, X, owned)),
        dma((2, 2, X, owned)),
        dma((2, 2, X, owned)),
        dma((2, B, N)),
        dma((2, B, N)),
        dma((B, N)),
        dma((B, N)),
        dma((B, N)),
        dma((B, N)),
        dma((2, 2, row)),
        dma((2, 2, row)),
        dma((2, max(X - 1, 1), owned)),
        dma((2, max(X - 1, 1), owned)),
    ]
    any_spec = pl.BlockSpec(memory_space=pl.ANY)
    vmem = pl.BlockSpec(memory_space=pltpu.VMEM)
    smem = pl.BlockSpec(memory_space=pltpu.SMEM)
    return pl.pallas_call(
        functools.partial(kernel, (Z, X, B)),
        out_shape=(
            pltpu.VMEM(templates.shape, f32),
            pltpu.VMEM(exposures.shape, f32),
        ),
        in_specs=[any_spec] * 3 + [smem] * 4,
        out_specs=(vmem, vmem),
        scratch_shapes=scratch,
        compiler_params=pltpu.CompilerParams(
            collective_id=0, has_side_effects=True, vmem_limit_bytes=56 * 2**20
        ),
    )(
        templates,
        exposures,
        variance,
        coefficients,
        jnp.swapaxes(psf_width, 2, 3),
        patch_ids,
        live_count,
    )


def solution(mesh):
    in_specs = (
        P(("groups", "exp"), "patch", None, "band"),
        P(("groups", "exp"), "patch", None, None, "band"),
        P(("groups", "exp"), "patch", None, None, "band"),
        P(("groups", "exp"), "patch", None, None),
        P(("groups", "exp"), "patch", None, None),
        P(("groups", "exp"), "patch", None),
        P(("groups", "exp"), "patch"),
    )
    out_specs = (
        P(("groups", "exp"), "patch", None, "band"),
        P(("groups", "exp"), "patch", None, None, "band"),
    )
    return jax.shard_map(
        on_device, mesh=mesh, in_specs=in_specs, out_specs=out_specs, check_vma=False
    )
```

```python
import functools

import jax
import jax.numpy as jnp
import numpy as np
from jax import lax
from jax.experimental import pallas as pl
from jax.experimental.pallas import tpu as pltpu
from jax.sharding import PartitionSpec as P

HW = 10
PW = 7
PARTS = 4

sigmas = (0.75, 1.5, 3.0)
degrees = (4, 2, 2)
starts = (0, 5, 8)
profiles = [(group, power) for group in range(3) for power in range(degrees[group] + 1)]

MESH = pl.DeviceIdType.MESH


def scale_of(group, power):
    grid = np.arange(-HW, HW + 1).astype(np.float64)
    base = np.exp(-grid * grid / (2.0 * sigmas[group] ** 2)) * (grid / HW) ** power
    return float(1.0 / np.sqrt(np.sum(base * base)))


def profile_tables(offset):
    spot = offset.astype(jnp.float32)
    inside = jnp.abs(offset) <= HW
    ratio = spot * (1.0 / HW)
    tables = []
    for group in range(3):
        value = jnp.exp(spot * spot * (-0.5 / sigmas[group] ** 2))
        value = jnp.where(inside, value, 0.0)
        for power in range(degrees[group] + 1):
            tables.append(value * scale_of(group, power))
            value = value * ratio
    return tables


def point_table(offset, width):
    rate = -0.5 / (width * width)
    total = 1.0 + 2.0 * sum(jnp.exp(rate * float(u * u)) for u in range(1, PW + 1))
    spot = offset.astype(jnp.float32)
    value = jnp.exp(spot * spot * rate) * (1.0 / total)
    return jnp.where(jnp.abs(offset) <= PW, value, 0.0)


def offsets(rows, cols, shift):
    row = lax.broadcasted_iota(jnp.int32, (rows, cols), 0)
    col = lax.broadcasted_iota(jnp.int32, (rows, cols), 1)
    return col - row + shift


def kernel(
    sizes,
    templates,
    exposures,
    variance,
    coeff,
    psf,
    ids,
    live,
    coadd,
    score,
    win0,
    win1,
    win2,
    win3,
    tfull,
    mats,
    gcat,
    gtab,
    cols,
    expo,
    inv,
    wval,
    wfull,
    ifull,
    rden,
    prow,
    qrow,
    pcol,
    qcol,
    psend,
    precv,
    pown,
    xsend,
    xrecv,
    local_sem,
    var_sem,
    exp_sem,
    xs_sem,
    xr_sem,
    zs_sem,
    zr_sem,
    ts_sem,
    tr_sem,
    is_sem,
    ir_sem,
    ws_sem,
    wr_sem,
    ps_sem,
    pr_sem,
    ss_sem,
    sr_sem,
):
    Z, X, B = sizes
    owned, S, C = templates.shape[1:]
    slots = ids.shape[2]
    N = ids.shape[1] * slots
    row_patches = X * owned
    z = lax.axis_index("exp")
    x = lax.axis_index("patch")
    b = lax.axis_index("band")

    def column(o):
        return lax.rem(x + o, X)

    def back_column(o):
        return lax.rem(x + X - o, X)

    def other_band(o):
        return lax.rem(b + o, B)

    def back_band(o):
        return lax.rem(b + B - o, B)

    to_exists = (z > 0, z < Z - 1)
    from_exists = (z < Z - 1, z > 0)
    target = (z - 1, z + 1)
    lands = (2, 0)

    def remote(src, dst, send, recv, device):
        return pltpu.make_async_remote_copy(
            src_ref=src,
            dst_ref=dst,
            send_sem=send,
            recv_sem=recv,
            device_id=device,
            device_id_type=MESH,
        )

    barrier = pltpu.get_barrier_semaphore()
    for d in range(2):

        @pl.when(to_exists[d])
        def _():
            pl.semaphore_signal(barrier, inc=1, device_id={"exp": target[d]}, device_id_type=MESH)

    for o in range(1, X):
        pl.semaphore_signal(barrier, inc=1, device_id={"patch": column(o)}, device_id_type=MESH)
    for o in range(1, B):
        pl.semaphore_signal(barrier, inc=1, device_id={"band": other_band(o)}, device_id_type=MESH)

    H = S // PARTS
    win = (win0, win1, win2, win3)
    edges = [0] + [h * H - 16 for h in range(1, PARTS)] + [S]
    bounds = list(zip(edges[:-1], edges[1:]))
    pair = 2 if owned % 2 == 0 else 1

    def var_copy(n):
        return pltpu.make_async_copy(
            variance.at[0, n // slots, lax.rem(n, slots)], inv.at[n], var_sem.at[n]
        )

    def exp_copy(n):
        return pltpu.make_async_copy(
            exposures.at[0, n // slots, lax.rem(n, slots)], expo.at[n], exp_sem.at[n]
        )

    def own_copy(h):
        return pltpu.make_async_copy(
            templates.at[0, :, pl.ds(h * H, H)],
            win[h].at[pl.ds(row_patches + x * owned, owned)],
            local_sem.at[h],
        )

    def start_local(n, carry):
        var_copy(n).start()
        return carry

    lax.fori_loop(0, N, start_local, 0)
    pl.semaphore_wait(
        barrier,
        (z > 0).astype(jnp.int32) + (z < Z - 1).astype(jnp.int32) + (X - 1) + (B - 1),
    )

    def block(h):
        return templates.at[0, :, pl.ds(h * H, H)]

    def place(h, row, o):
        return win[h].at[pl.ds(row * row_patches + column(o) * owned, owned)]

    def x_copy(h, o):
        return remote(
            block(h),
            place(h, 1, 0),
            xs_sem.at[h, o],
            xr_sem.at[h, o],
            {"patch": back_column(o)},
        )

    def z_copy(h, d, o):
        return remote(
            block(h) if o == 0 else place(h, 1, o),
            place(h, lands[d], o),
            zs_sem.at[h, d, o],
            zr_sem.at[h, d, o],
            {"exp": target[d]},
        )

    def launch(h):
        for o in range(1, X):
            x_copy(h, o).start()
        for d in range(2):

            @pl.when(to_exists[d])
            def _():
                z_copy(h, d, 0).start()

    def forward(h):
        for o in range(1, X):
            x_copy(h, o).wait_recv()
            for d in range(2):

                @pl.when(to_exists[d])
                def _():
                    z_copy(h, d, o).start()

    def half_copy(buffer, send, recv, o, n):
        return remote(
            buffer.at[n, :, 0:C],
            buffer.at[n, :, o * C : (o + 1) * C],
            send.at[o, n],
            recv.at[o, n],
            {"band": back_band(o)},
        )

    def invert(n, carry):
        var_copy(n).wait()
        weight = 1.0 / inv[n]
        inv[n] = weight
        ifull[n, :, 0:C] = weight.astype(jnp.bfloat16)
        for o in range(1, B):
            half_copy(ifull, is_sem, ir_sem, o, n).start()
        return carry

    launch(0)
    launch(1)

    def start_exposure(n, carry):
        exp_copy(n).start()
        return carry

    lax.fori_loop(0, N, start_exposure, 0)
    for h in range(PARTS):
        own_copy(h).start()
    lax.fori_loop(0, N, invert, 0)
    forward(0)
    launch(2)

    count = len(profiles) + len(profiles) % 2
    gcat[...] = jnp.zeros((S, PARTS * count * H), jnp.bfloat16)
    row = lax.broadcasted_iota(jnp.int32, (H + 32, 2 * H), 0)
    lane = lax.broadcasted_iota(jnp.int32, (H + 32, 2 * H), 1)
    first_half = lane < H
    tables = profile_tables(row - 16 - jnp.where(first_half, lane, lane - H))
    tables = tables + [jnp.zeros_like(tables[0])] * (count - len(tables))
    for p in range(0, count, 2):
        table = jnp.where(first_half, tables[p], tables[p + 1]).astype(jnp.bfloat16)
        for h in range(PARTS):
            first, last = max(h * H - 16, 0), min((h + 1) * H + 16, S)
            lanes = slice((h * count + p) * H, (h * count + p + 2) * H)
            gcat[first:last, lanes] = table[first - h * H + 16 : last - h * H + 16]
    shifts = [(b - other_band(o)) * C for o in range(B)]
    for p, table in enumerate(profile_tables(offsets(C, C, 0))):
        gtab[p, 0:C, :] = table
    for o in range(1, B):
        start = C + (o - 1) * 32
        for p, table in enumerate(profile_tables(offsets(16, C, shifts[o]))):
            gtab[p, start : start + 16, :] = table
        for p, table in enumerate(profile_tables(offsets(16, C, shifts[o] - C + 16))):
            gtab[p, start + 16 : start + 32, :] = table

    def mix(n, carry):
        e, k = n // slots, lax.rem(n, slots)
        if B > 1:
            mats[n, C : B * C, :] = jnp.zeros(((B - 1) * C, count * C), jnp.bfloat16)
        index = 0
        for p, (group, power) in enumerate(profiles):
            value = coeff[0, e, k, index] * gtab[starts[group]]
            index += 1
            for j in range(1, degrees[group] + 1 - power):
                value = value + coeff[0, e, k, index] * gtab[starts[group] + j]
                index += 1
            value = value.astype(jnp.bfloat16)
            lanes = slice(p * C, (p + 1) * C)
            mats[n, 0:C, lanes] = value[0:C]
            for o in range(1, B):
                start = C + (o - 1) * 32
                mats[n, o * C : o * C + 16, lanes] = value[start : start + 16]
                mats[n, (o + 1) * C - 16 : (o + 1) * C, lanes] = value[start + 16 : start + 32]
        spare = count - len(profiles)
        if spare:
            mats[n, 0:C, (count - spare) * C :] = jnp.zeros((C, spare * C), jnp.bfloat16)
        return carry

    forward(1)
    launch(3)
    lax.fori_loop(0, N, mix, 0)
    forward(2)

    for d in range(2):

        @pl.when(jnp.logical_not(from_exists[d]))
        def _():
            for h in range(PARTS):

                def clear(i, carry):
                    win[h][lands[d] * row_patches + i] = jnp.zeros((H, C), jnp.bfloat16)
                    return carry

                lax.fori_loop(0, row_patches, clear, 0)

    def spread(n, carry):
        e, k = n // slots, lax.rem(n, slots)

        def put(low, square, rows, lanes, table):
            low[n, rows, lanes] = table.astype(jnp.bfloat16)
            square[n, rows, lanes] = (table * table).astype(jnp.bfloat16)

        half = S // 2
        width = jnp.full((1, half), psf[0, e, 0, k], jnp.float32)
        prow[n] = jnp.zeros((S, S), jnp.bfloat16)
        qrow[n] = jnp.zeros((S, S), jnp.bfloat16)
        low, high = slice(0, half), slice(half, S)
        table = point_table(offsets(half, half, 0), width)
        put(prow, qrow, low, low, table)
        put(prow, qrow, high, high, table)
        table = point_table(offsets(16, half, -half), width)
        put(prow, qrow, slice(half, half + 16), low, table)
        table = point_table(offsets(16, half, 16), width)
        put(prow, qrow, slice(half - 16, half), high, table)
        width = jnp.full((1, C), psf[0, e, 1, k], jnp.float32)
        pcol[n] = jnp.zeros((B * C, C), jnp.bfloat16)
        qcol[n] = jnp.zeros((B * C, C), jnp.bfloat16)
        lanes = slice(0, C)
        put(pcol, qcol, slice(0, C), lanes, point_table(offsets(C, C, 0), width))
        for o in range(1, B):
            first, last = o * C, (o + 1) * C
            table = point_table(offsets(16, C, shifts[o]), width)
            put(pcol, qcol, slice(first, first + 16), lanes, table)
            table = point_table(offsets(16, C, shifts[o] - C + 16), width)
            put(pcol, qcol, slice(last - 16, last), lanes, table)
        return carry

    def alive_of(n):
        e, k = n // slots, lax.rem(n, slots)
        return jnp.where(k < live[0, e], 1.0, 0.0).astype(jnp.float32)

    def matched(chains):
        middle = [
            jnp.dot(rows, full, preferred_element_type=jnp.float32).astype(jnp.bfloat16)
            for rows, full, _ in chains
        ]
        return [
            jnp.dot(part, chain[2], preferred_element_type=jnp.float32)
            for part, chain in zip(middle, chains)
        ]

    def denominator(pair, carry):
        tiles = (pair * 2, pair * 2 + 1)
        for n in tiles:
            for o in range(1, B):
                half_copy(ifull, is_sem, ir_sem, o, n).wait_recv()
        results = matched([(qrow[n], ifull[n], qcol[n]) for n in tiles])
        for n, result in zip(tiles, results):
            rden[n] = lax.rsqrt(result) * alive_of(n)
        return carry

    def arrive(h):
        own_copy(h).wait()
        for d in range(2):

            @pl.when(from_exists[d])
            def _():
                for o in range(X):
                    z_copy(h, d, o).wait_recv()

    def tile_copy(h, o, n):
        return remote(
            tfull.at[h, n, :, 0:C],
            tfull.at[h, n, :, o * C : (o + 1) * C],
            ts_sem.at[h, o, n],
            tr_sem.at[h, o, n],
            {"band": back_band(o)},
        )

    def middle(h):
        first, last = bounds[h]
        start, end = max(h - 1, 0) * count * H, (h + 1) * count * H

        def choose(n, carry):
            tfull[h, n, :, 0:C] = win[h][ids[0, n // slots, lax.rem(n, slots)]]
            for o in range(1, B):
                tile_copy(h, o, n).start()
            return carry

        lax.fori_loop(0, N, choose, 0)

        def convolve(pair, carry):
            for a in range(2):
                n = pair * 2 + a
                if h == 0:
                    exp_copy(n).wait()
                for o in range(1, B):
                    tile_copy(h, o, n).wait_recv()
                tile = tfull[h, n]
                for p in range(0, count, 2):
                    wide = min(2, count - p)
                    part = jnp.dot(
                        tile,
                        mats[n, :, p * C : (p + wide) * C],
                        preferred_element_type=jnp.float32,
                    ).astype(jnp.bfloat16)
                    for v in range(wide):
                        row = (h * count + p + v) * H
                        cols[pair, row : row + H, a * C : (a + 1) * C] = part[
                            :, v * C : (v + 1) * C
                        ]
            convolved = jnp.dot(
                gcat[first:last, start:end],
                cols[pair, start:end, :],
                preferred_element_type=jnp.float32,
            )
            for a in range(2):
                n = pair * 2 + a
                value = expo[n, first:last, :].astype(jnp.float32)
                value = (value - convolved[:, a * C : (a + 1) * C]) * inv[n, first:last, :]
                wval[n, first:last, :] = value
                wfull[n, first:last, 0:C] = value.astype(jnp.bfloat16)
                if h == PARTS - 1:
                    for o in range(1, B):
                        half_copy(wfull, ws_sem, wr_sem, o, n).start()
            return carry

        lax.fori_loop(0, N // 2, convolve, 0)

    def partials(h, q, rows):
        first, last = bounds[h]
        factors = []
        for row in rows:
            hits = []
            for n in range(N):
                e, k = n // slots, n % slots
                hit = jnp.logical_and(ids[0, e, k] == row * row_patches + q, k < live[0, e])
                hits.append(jnp.where(hit, 1.0, 0.0).astype(jnp.float32))
            factors.append(hits)
        step = 16
        for start in range(first, last, step):
            values = [jnp.zeros((step, C), jnp.float32) for _ in rows]
            for n in range(N):
                tile = wval[n, start : start + step, :]
                values = [value + hits[n] * tile for value, hits in zip(values, factors)]
            yield slice(start, start + step), values

    def p_copy(h, d, q, t):
        first, last = bounds[h]
        part = (d, pl.ds(q, pair), pl.ds(first, last - first))
        return remote(
            psend.at[part],
            precv.at[part],
            ps_sem.at[h, d, t],
            pr_sem.at[h, d, t],
            {"exp": target[d]},
        )

    def patch_of(t):
        per = owned // pair
        return lax.rem(x + 1 + t // per, X) * owned + lax.rem(t, per) * pair

    def push(h):
        def step(t, carry):
            for v in range(pair):
                q = patch_of(t) + v
                for rows, (up, own, down) in partials(h, q, (0, 1, 2)):
                    psend[0, q, rows, :] = up.astype(jnp.bfloat16)
                    psend[1, q, rows, :] = down.astype(jnp.bfloat16)
                    pown[q, rows, :] = own
            for d in range(2):

                @pl.when(to_exists[d])
                def _():
                    p_copy(h, d, patch_of(t), t).start()

            return carry

        lax.fori_loop(0, row_patches // pair, step, 0)

    def numerator(pair, carry):
        tiles = (pair * 2, pair * 2 + 1)
        for n in tiles:
            for o in range(1, B):
                half_copy(wfull, ws_sem, wr_sem, o, n).wait_recv()
        results = matched([(prow[n], wfull[n], pcol[n]) for n in tiles])
        for n, result in zip(tiles, results):
            score[0, n // slots, lax.rem(n, slots)] = result * rden[n]
        return carry

    def gather_rows(h, o):
        first, last = bounds[h]
        for i in range(0, owned, pair):
            t = ((o + X - 1) % X) * (owned // pair) + i // pair
            q = column(o) * owned + i
            for d in range(2):

                @pl.when(from_exists[d])
                def _():
                    p_copy(h, d, q, t).wait_recv()
                    for v in range(pair):
                        extra = precv[d, q + v, first:last, :].astype(jnp.float32)
                        pown[q + v, first:last, :] += extra

    def s_copy(h, s):
        first, last = bounds[h]
        rows = pl.ds(first, last - first)
        return remote(
            xsend.at[s, :, rows],
            xrecv.at[s, :, rows],
            ss_sem.at[h, s],
            sr_sem.at[h, s],
            {"patch": column(s + 1)},
        )

    def pass_on(h):
        first, last = bounds[h]
        for s in range(X - 1):
            gather_rows(h, s + 1)
            for i in range(owned):
                q = column(s + 1) * owned + i
                xsend[s, i, first:last, :] = pown[q, first:last, :].astype(jnp.bfloat16)
            s_copy(h, s).start()

    def finish_sums(h):
        first, last = bounds[h]
        gather_rows(h, 0)
        for s in range(X - 1):
            s_copy(h, s).wait_recv()
        for i in range(owned):
            value = pown[x * owned + i, first:last, :]
            for s in range(X - 1):
                value = value + xrecv[s, i, first:last, :].astype(jnp.float32)
            coadd[0, i, first:last, :] = value

    arrive(0)
    middle(0)
    push(0)
    forward(3)
    lax.fori_loop(0, N // 2, spread, 0)
    arrive(1)
    middle(1)
    push(1)
    pass_on(0)
    lax.fori_loop(N // 2, N, spread, 0)
    arrive(2)
    middle(2)
    push(2)
    pass_on(1)
    finish_sums(0)
    arrive(3)
    middle(3)
    push(3)
    pass_on(2)
    lax.fori_loop(0, N // 2, denominator, 0)
    pass_on(3)
    finish_sums(1)
    finish_sums(2)
    lax.fori_loop(0, N // 2, numerator, 0)
    finish_sums(3)

    for h in range(PARTS):
        for o in range(1, X):
            x_copy(h, o).wait_send()
            s_copy(h, o - 1).wait_send()
        for d in range(2):

            @pl.when(to_exists[d])
            def _():
                for o in range(X):
                    z_copy(h, d, o).wait_send()

                def sent(t, carry):
                    p_copy(h, d, patch_of(t), t).wait_send()
                    return carry

                lax.fori_loop(0, row_patches // pair, sent, 0)

    def finish(n, carry):
        for o in range(1, B):
            half_copy(ifull, is_sem, ir_sem, o, n).wait_send()
            half_copy(wfull, ws_sem, wr_sem, o, n).wait_send()
            for h in range(PARTS):
                tile_copy(h, o, n).wait_send()
        return carry

    lax.fori_loop(0, N, finish, 0)


def on_device(templates, exposures, variance, coefficients, psf_width, patch_ids, live_count):
    owned, S, C = templates.shape[1:]
    Z, X, B = (lax.axis_size(axis) for axis in ("exp", "patch", "band"))
    N = patch_ids.shape[1] * patch_ids.shape[2]
    row = X * owned
    count = len(profiles) + len(profiles) % 2
    bf16, f32 = jnp.bfloat16, jnp.float32
    dma = pltpu.SemaphoreType.DMA
    scratch = [
        *[pltpu.VMEM((3 * row, S // PARTS, C), bf16) for _ in range(PARTS)],
        pltpu.VMEM((PARTS, N, S // PARTS, B * C), bf16),
        pltpu.VMEM((N, B * C, count * C), bf16),
        pltpu.VMEM((S, count * S), bf16),
        pltpu.VMEM((count, C + 32 * (B - 1), C), f32),
        pltpu.VMEM((N // 2, count * S, 2 * C), bf16),
        pltpu.VMEM((N, S, C), bf16),
        pltpu.VMEM((N, S, C), f32),
        pltpu.VMEM((N, S, C), f32),
        pltpu.VMEM((N, S, B * C), bf16),
        pltpu.VMEM((N, S, B * C), bf16),
        pltpu.VMEM((N, S, C), f32),
        pltpu.VMEM((N, S, S), bf16),
        pltpu.VMEM((N, S, S), bf16),
        pltpu.VMEM((N, B * C, C), bf16),
        pltpu.VMEM((N, B * C, C), bf16),
        pltpu.VMEM((2, row, S, C), bf16),
        pltpu.VMEM((2, row, S, C), bf16),
        pltpu.VMEM((row, S, C), f32),
        pltpu.VMEM((max(X - 1, 1), owned, S, C), bf16),
        pltpu.VMEM((max(X - 1, 1), owned, S, C), bf16),
        dma((PARTS,)),
        dma((N,)),
        dma((N,)),
        dma((PARTS, X)),
        dma((PARTS, X)),
        dma((PARTS, 2, X)),
        dma((PARTS, 2, X)),
        dma((PARTS, B, N)),
        dma((PARTS, B, N)),
        dma((B, N)),
        dma((B, N)),
        dma((B, N)),
        dma((B, N)),
        dma((PARTS, 2, row)),
        dma((PARTS, 2, row)),
        dma((PARTS, max(X - 1, 1))),
        dma((PARTS, max(X - 1, 1))),
    ]
    any_spec = pl.BlockSpec(memory_space=pl.ANY)
    vmem = pl.BlockSpec(memory_space=pltpu.VMEM)
    smem = pl.BlockSpec(memory_space=pltpu.SMEM)
    return pl.pallas_call(
        functools.partial(kernel, (Z, X, B)),
        out_shape=(
            pltpu.VMEM(templates.shape, f32),
            pltpu.VMEM(exposures.shape, f32),
        ),
        in_specs=[any_spec] * 3 + [smem] * 4,
        out_specs=(vmem, vmem),
        scratch_shapes=scratch,
        compiler_params=pltpu.CompilerParams(
            collective_id=0, has_side_effects=True, vmem_limit_bytes=56 * 2**20
        ),
    )(
        templates,
        exposures,
        variance,
        coefficients,
        jnp.swapaxes(psf_width, 2, 3),
        patch_ids,
        live_count,
    )


def solution(mesh):
    in_specs = (
        P(("groups", "exp"), "patch", None, "band"),
        P(("groups", "exp"), "patch", None, None, "band"),
        P(("groups", "exp"), "patch", None, None, "band"),
        P(("groups", "exp"), "patch", None, None),
        P(("groups", "exp"), "patch", None, None),
        P(("groups", "exp"), "patch", None),
        P(("groups", "exp"), "patch"),
    )
    out_specs = (
        P(("groups", "exp"), "patch", None, "band"),
        P(("groups", "exp"), "patch", None, None, "band"),
    )
    return jax.shard_map(
        on_device, mesh=mesh, in_specs=in_specs, out_specs=out_specs, check_vma=False
    )
```

```python
import functools

import jax
import jax.numpy as jnp
import numpy as np
from jax import lax
from jax.experimental import pallas as pl
from jax.experimental.pallas import tpu as pltpu
from jax.sharding import PartitionSpec as P

HW = 10
PW = 7

sigmas = (0.75, 1.5, 3.0)
degrees = (4, 2, 2)
starts = (0, 5, 8)
profiles = [(group, power) for group in range(3) for power in range(degrees[group] + 1)]

MESH = pl.DeviceIdType.MESH


def scale_of(group, power):
    grid = np.arange(-HW, HW + 1).astype(np.float64)
    base = np.exp(-grid * grid / (2.0 * sigmas[group] ** 2)) * (grid / HW) ** power
    return float(1.0 / np.sqrt(np.sum(base * base)))


def profile_tables(offset):
    spot = offset.astype(jnp.float32)
    inside = jnp.abs(offset) <= HW
    ratio = spot * (1.0 / HW)
    tables = []
    for group in range(3):
        value = jnp.exp(spot * spot * (-0.5 / sigmas[group] ** 2))
        value = jnp.where(inside, value, 0.0)
        for power in range(degrees[group] + 1):
            tables.append(value * scale_of(group, power))
            value = value * ratio
    return tables


def point_table(offset, width):
    rate = -0.5 / (width * width)
    total = 1.0 + 2.0 * sum(jnp.exp(rate * float(u * u)) for u in range(1, PW + 1))
    spot = offset.astype(jnp.float32)
    value = jnp.exp(spot * spot * rate) * (1.0 / total)
    return jnp.where(jnp.abs(offset) <= PW, value, 0.0)


def offsets(rows, cols, shift):
    row = lax.broadcasted_iota(jnp.int32, (rows, cols), 0)
    col = lax.broadcasted_iota(jnp.int32, (rows, cols), 1)
    return col - row + shift


def kernel(
    sizes,
    templates,
    exposures,
    variance,
    coeff,
    psf,
    ids,
    live,
    coadd,
    score,
    win0,
    win1,
    tfull,
    mats,
    gcat,
    gtab,
    cols,
    expo,
    inv,
    wval,
    wfull,
    ifull,
    rden,
    prow,
    qrow,
    pcol,
    qcol,
    psend,
    precv,
    pown,
    xsend,
    xrecv,
    local_sem,
    var_sem,
    exp_sem,
    xs_sem,
    xr_sem,
    zs_sem,
    zr_sem,
    ts_sem,
    tr_sem,
    is_sem,
    ir_sem,
    ws_sem,
    wr_sem,
    ps_sem,
    pr_sem,
    ss_sem,
    sr_sem,
):
    Z, X, B = sizes
    owned, S, C = templates.shape[1:]
    slots = ids.shape[2]
    N = ids.shape[1] * slots
    row_patches = X * owned
    z = lax.axis_index("exp")
    x = lax.axis_index("patch")
    b = lax.axis_index("band")

    def column(o):
        return lax.rem(x + o, X)

    def back_column(o):
        return lax.rem(x + X - o, X)

    def other_band(o):
        return lax.rem(b + o, B)

    def back_band(o):
        return lax.rem(b + B - o, B)

    to_exists = (z > 0, z < Z - 1)
    from_exists = (z < Z - 1, z > 0)
    target = (z - 1, z + 1)
    lands = (2, 0)

    def remote(src, dst, send, recv, device):
        return pltpu.make_async_remote_copy(
            src_ref=src,
            dst_ref=dst,
            send_sem=send,
            recv_sem=recv,
            device_id=device,
            device_id_type=MESH,
        )

    barrier = pltpu.get_barrier_semaphore()
    for d in range(2):

        @pl.when(to_exists[d])
        def _():
            pl.semaphore_signal(barrier, inc=1, device_id={"exp": target[d]}, device_id_type=MESH)

    for o in range(1, X):
        pl.semaphore_signal(barrier, inc=1, device_id={"patch": column(o)}, device_id_type=MESH)
    for o in range(1, B):
        pl.semaphore_signal(barrier, inc=1, device_id={"band": other_band(o)}, device_id_type=MESH)

    H = S // 2
    win = (win0, win1)
    gs = max(owned // 2, 1)
    groups = owned // gs
    bounds = ((0, H - 16), (H - 16, S))

    def var_copy(n):
        return pltpu.make_async_copy(
            variance.at[0, n // slots, lax.rem(n, slots)], inv.at[n], var_sem.at[n]
        )

    def exp_copy(n):
        return pltpu.make_async_copy(
            exposures.at[0, n // slots, lax.rem(n, slots)], expo.at[n], exp_sem.at[n]
        )

    def own_copy(h):
        return pltpu.make_async_copy(
            templates.at[0, :, pl.ds(h * H, H)],
            win[h].at[pl.ds(row_patches + x * owned, owned)],
            local_sem.at[h],
        )

    def start_local(n, carry):
        var_copy(n).start()
        return carry

    lax.fori_loop(0, N, start_local, 0)
    pl.semaphore_wait(
        barrier,
        (z > 0).astype(jnp.int32) + (z < Z - 1).astype(jnp.int32) + (X - 1) + (B - 1),
    )

    def block(h, i):
        return templates.at[0, pl.ds(i * gs, gs), pl.ds(h * H, H)]

    def place(h, row, o, i):
        return win[h].at[pl.ds(row * row_patches + column(o) * owned + i * gs, gs)]

    def x_copy(h, o, i):
        return remote(
            block(h, i),
            place(h, 1, 0, i),
            xs_sem.at[h, o, i],
            xr_sem.at[h, o, i],
            {"patch": back_column(o)},
        )

    def z_copy(h, d, o, i):
        return remote(
            block(h, i) if o == 0 else place(h, 1, o, i),
            place(h, lands[d], o, i),
            zs_sem.at[h, d, o, i],
            zr_sem.at[h, d, o, i],
            {"exp": target[d]},
        )

    def launch(h):
        for i in range(groups):
            for o in range(1, X):
                x_copy(h, o, i).start()
            for d in range(2):

                @pl.when(to_exists[d])
                def _():
                    z_copy(h, d, 0, i).start()

    def forward(h):
        for i in range(groups):
            for o in range(1, X):
                x_copy(h, o, i).wait_recv()
                for d in range(2):

                    @pl.when(to_exists[d])
                    def _():
                        z_copy(h, d, o, i).start()

    def half_copy(buffer, send, recv, o, n):
        return remote(
            buffer.at[n, :, 0:C],
            buffer.at[n, :, o * C : (o + 1) * C],
            send.at[o, n],
            recv.at[o, n],
            {"band": back_band(o)},
        )

    def invert(n, carry):
        var_copy(n).wait()
        weight = 1.0 / inv[n]
        inv[n] = weight
        ifull[n, :, 0:C] = weight.astype(jnp.bfloat16)
        for o in range(1, B):
            half_copy(ifull, is_sem, ir_sem, o, n).start()
        return carry

    launch(0)

    def start_exposure(n, carry):
        exp_copy(n).start()
        return carry

    lax.fori_loop(0, N, start_exposure, 0)
    for h in range(2):
        own_copy(h).start()
    lax.fori_loop(0, N // 2, invert, 0)
    forward(0)
    launch(1)
    lax.fori_loop(N // 2, N, invert, 0)

    count = len(profiles)
    gcat[...] = jnp.zeros((S, 2 * count * H), jnp.bfloat16)
    for p, table in enumerate(profile_tables(-offsets(H, H, 0))):
        table = table.astype(jnp.bfloat16)
        gcat[0:H, p * H : (p + 1) * H] = table
        gcat[H:S, (count + p) * H : (count + p + 1) * H] = table
    for p, table in enumerate(profile_tables(-offsets(16, H, -H))):
        gcat[H : H + 16, p * H : (p + 1) * H] = table.astype(jnp.bfloat16)
    for p, table in enumerate(profile_tables(-offsets(16, H, 16))):
        gcat[H - 16 : H, (count + p) * H : (count + p + 1) * H] = table.astype(jnp.bfloat16)
    shifts = [(b - other_band(o)) * C for o in range(B)]
    for p, table in enumerate(profile_tables(offsets(C, C, 0))):
        gtab[p, 0:C, :] = table
    for o in range(1, B):
        start = C + (o - 1) * 32
        for p, table in enumerate(profile_tables(offsets(16, C, shifts[o]))):
            gtab[p, start : start + 16, :] = table
        for p, table in enumerate(profile_tables(offsets(16, C, shifts[o] - C + 16))):
            gtab[p, start + 16 : start + 32, :] = table

    def mix(n, carry):
        e, k = n // slots, lax.rem(n, slots)
        if B > 1:
            mats[n, C : B * C, :] = jnp.zeros(((B - 1) * C, count * C), jnp.bfloat16)
        index = 0
        for p, (group, power) in enumerate(profiles):
            value = coeff[0, e, k, index] * gtab[starts[group]]
            index += 1
            for j in range(1, degrees[group] + 1 - power):
                value = value + coeff[0, e, k, index] * gtab[starts[group] + j]
                index += 1
            value = value.astype(jnp.bfloat16)
            lanes = slice(p * C, (p + 1) * C)
            mats[n, 0:C, lanes] = value[0:C]
            for o in range(1, B):
                start = C + (o - 1) * 32
                mats[n, o * C : o * C + 16, lanes] = value[start : start + 16]
                mats[n, (o + 1) * C - 16 : (o + 1) * C, lanes] = value[start + 16 : start + 32]
        return carry

    lax.fori_loop(0, N, mix, 0)
    forward(1)

    for d in range(2):

        @pl.when(jnp.logical_not(from_exists[d]))
        def _():
            for h in range(2):

                def clear(i, carry):
                    win[h][lands[d] * row_patches + i] = jnp.zeros((H, C), jnp.bfloat16)
                    return carry

                lax.fori_loop(0, row_patches, clear, 0)

    def spread(n, carry):
        e, k = n // slots, lax.rem(n, slots)

        def put(low, square, rows, lanes, table):
            low[n, rows, lanes] = table.astype(jnp.bfloat16)
            square[n, rows, lanes] = (table * table).astype(jnp.bfloat16)

        width = jnp.full((1, H), psf[0, e, 0, k], jnp.float32)
        prow[n] = jnp.zeros((S, S), jnp.bfloat16)
        qrow[n] = jnp.zeros((S, S), jnp.bfloat16)
        table = point_table(offsets(H, H, 0), width)
        put(prow, qrow, slice(0, H), slice(0, H), table)
        put(prow, qrow, slice(H, S), slice(H, S), table)
        put(prow, qrow, slice(H, H + 16), slice(0, H), point_table(offsets(16, H, -H), width))
        put(prow, qrow, slice(H - 16, H), slice(H, S), point_table(offsets(16, H, 16), width))
        width = jnp.full((1, C), psf[0, e, 1, k], jnp.float32)
        pcol[n] = jnp.zeros((B * C, C), jnp.bfloat16)
        qcol[n] = jnp.zeros((B * C, C), jnp.bfloat16)
        lanes = slice(0, C)
        put(pcol, qcol, slice(0, C), lanes, point_table(offsets(C, C, 0), width))
        for o in range(1, B):
            first, last = o * C, (o + 1) * C
            table = point_table(offsets(16, C, shifts[o]), width)
            put(pcol, qcol, slice(first, first + 16), lanes, table)
            table = point_table(offsets(16, C, shifts[o] - C + 16), width)
            put(pcol, qcol, slice(last - 16, last), lanes, table)
        return carry

    def alive_of(n):
        e, k = n // slots, lax.rem(n, slots)
        return jnp.where(k < live[0, e], 1.0, 0.0).astype(jnp.float32)

    def matched(chains):
        middle = [
            jnp.dot(rows, full, preferred_element_type=jnp.float32).astype(jnp.bfloat16)
            for rows, full, _ in chains
        ]
        return [
            jnp.dot(part, chain[2], preferred_element_type=jnp.float32)
            for part, chain in zip(middle, chains)
        ]

    def denominator(step, carry):
        tiles = [step * 4 + a for a in range(4)]
        for n in tiles:
            for o in range(1, B):
                half_copy(ifull, is_sem, ir_sem, o, n).wait_recv()
        results = matched([(qrow[n], ifull[n], qcol[n]) for n in tiles])
        for n, result in zip(tiles, results):
            rden[n] = lax.rsqrt(result) * alive_of(n)
        return carry

    def arrive(h):
        own_copy(h).wait()
        for d in range(2):

            @pl.when(from_exists[d])
            def _():
                for o in range(X):
                    for i in range(groups):
                        z_copy(h, d, o, i).wait_recv()

    def tile_copy(h, o, n):
        return remote(
            tfull.at[h, n, :, 0:C],
            tfull.at[h, n, :, o * C : (o + 1) * C],
            ts_sem.at[h, o, n],
            tr_sem.at[h, o, n],
            {"band": back_band(o)},
        )

    def middle(h):
        first, last = bounds[h]
        depth = (h + 1) * count * H

        def choose(n, carry):
            tfull[h, n, :, 0:C] = win[h][ids[0, n // slots, lax.rem(n, slots)]]
            for o in range(1, B):
                tile_copy(h, o, n).start()
            return carry

        for n in range(N):
            choose(n, 0)
        for n in range(N):
            if h == 0:
                exp_copy(n).wait()
            for o in range(1, B):
                tile_copy(h, o, n).wait_recv()
            tile = tfull[h, n]
            pair, a = n // 2, n % 2
            for p in range(0, count, 2):
                wide = min(2, count - p)
                part = jnp.dot(
                    tile,
                    mats[n, :, p * C : (p + wide) * C],
                    preferred_element_type=jnp.float32,
                ).astype(jnp.bfloat16)
                for v in range(wide):
                    row = (h * count + p + v) * H
                    cols[pair, row : row + H, a * C : (a + 1) * C] = part[:, v * C : (v + 1) * C]
        for pair in range(N // 2):
            convolved = jnp.dot(
                gcat[first:last, 0:depth],
                cols[pair, 0:depth, :],
                preferred_element_type=jnp.float32,
            )
            for a in range(2):
                n = pair * 2 + a
                value = expo[n, first:last, :].astype(jnp.float32)
                value = (value - convolved[:, a * C : (a + 1) * C]) * inv[n, first:last, :]
                wval[n, first:last, :] = value
                wfull[n, first:last, 0:C] = value.astype(jnp.bfloat16)
                if h == 1:
                    for o in range(1, B):
                        half_copy(wfull, ws_sem, wr_sem, o, n).start()

    def partials(h, q, rows):
        first, last = bounds[h]
        factors = []
        for row in rows:
            hits = []
            for n in range(N):
                e, k = n // slots, n % slots
                hit = jnp.logical_and(ids[0, e, k] == row * row_patches + q, k < live[0, e])
                hits.append(jnp.where(hit, 1.0, 0.0).astype(jnp.float32))
            factors.append(hits)
        step = 16
        for start in range(first, last, step):
            values = [jnp.zeros((step, C), jnp.float32) for _ in rows]
            for n in range(N):
                tile = wval[n, start : start + step, :]
                values = [value + hits[n] * tile for value, hits in zip(values, factors)]
            yield slice(start, start + step), values

    def p_copy(h, d, q, t):
        first, last = bounds[h]
        rows = pl.ds(first, last - first)
        return remote(
            psend.at[d, q, rows],
            precv.at[d, q, rows],
            ps_sem.at[h, d, t],
            pr_sem.at[h, d, t],
            {"exp": target[d]},
        )

    def patch_of(t):
        return lax.rem(x + 1 + t // owned, X) * owned + lax.rem(t, owned)

    def push(h):
        def step(t, carry):
            q = patch_of(t)
            for rows, (up, own, down) in partials(h, q, (0, 1, 2)):
                psend[0, q, rows, :] = up.astype(jnp.bfloat16)
                psend[1, q, rows, :] = down.astype(jnp.bfloat16)
                pown[q, rows, :] = own
            for d in range(2):

                @pl.when(to_exists[d])
                def _():
                    p_copy(h, d, q, t).start()

            return carry

        lax.fori_loop(0, row_patches, step, 0)

    def numerator(step, carry):
        tiles = [step * 4 + a for a in range(4)]
        for n in tiles:
            for o in range(1, B):
                half_copy(wfull, ws_sem, wr_sem, o, n).wait_recv()
        results = matched([(prow[n], wfull[n], pcol[n]) for n in tiles])
        for n, result in zip(tiles, results):
            score[0, n // slots, lax.rem(n, slots)] = result * rden[n]
        return carry

    def gather_rows(h, t, q):
        first, last = bounds[h]
        for d in range(2):

            @pl.when(from_exists[d])
            def _():
                p_copy(h, d, q, t).wait_recv()
                pown[q, first:last, :] += precv[d, q, first:last, :].astype(jnp.float32)

    def s_copy(h, s, i):
        first, last = bounds[h]
        rows = pl.ds(first, last - first)
        return remote(
            xsend.at[s, i, rows],
            xrecv.at[s, i, rows],
            ss_sem.at[h, s, i],
            sr_sem.at[h, s, i],
            {"patch": column(s + 1)},
        )

    def pass_on(h):
        first, last = bounds[h]
        for s in range(X - 1):
            for i in range(owned):
                q = column(s + 1) * owned + i
                gather_rows(h, s * owned + i, q)
                xsend[s, i, first:last, :] = pown[q, first:last, :].astype(jnp.bfloat16)
                s_copy(h, s, i).start()

    def finish_sums(h):
        first, last = bounds[h]
        for i in range(owned):
            q = x * owned + i
            gather_rows(h, (X - 1) * owned + i, q)
            value = pown[q, first:last, :]
            for s in range(X - 1):
                s_copy(h, s, i).wait_recv()
                value = value + xrecv[s, i, first:last, :].astype(jnp.float32)
            coadd[0, i, first:last, :] = value

    arrive(0)
    middle(0)
    push(0)
    arrive(1)
    middle(1)
    push(1)
    pass_on(0)
    lax.fori_loop(0, N, spread, 0)
    lax.fori_loop(0, N // 4, denominator, 0)
    pass_on(1)
    finish_sums(0)
    lax.fori_loop(0, N // 4, numerator, 0)
    finish_sums(1)

    for h in range(2):
        for o in range(1, X):
            for i in range(groups):
                x_copy(h, o, i).wait_send()
            for i in range(owned):
                s_copy(h, o - 1, i).wait_send()
        for d in range(2):

            @pl.when(to_exists[d])
            def _():
                for o in range(X):
                    for i in range(groups):
                        z_copy(h, d, o, i).wait_send()

                def sent(t, carry):
                    p_copy(h, d, patch_of(t), t).wait_send()
                    return carry

                lax.fori_loop(0, row_patches, sent, 0)

    def finish(n, carry):
        for o in range(1, B):
            half_copy(ifull, is_sem, ir_sem, o, n).wait_send()
            half_copy(wfull, ws_sem, wr_sem, o, n).wait_send()
            for h in range(2):
                tile_copy(h, o, n).wait_send()
        return carry

    lax.fori_loop(0, N, finish, 0)


def on_device(templates, exposures, variance, coefficients, psf_width, patch_ids, live_count):
    owned, S, C = templates.shape[1:]
    Z, X, B = (lax.axis_size(axis) for axis in ("exp", "patch", "band"))
    N = patch_ids.shape[1] * patch_ids.shape[2]
    row = X * owned
    count = len(profiles)
    bf16, f32 = jnp.bfloat16, jnp.float32
    dma = pltpu.SemaphoreType.DMA
    scratch = [
        pltpu.VMEM((3 * row, S // 2, C), bf16),
        pltpu.VMEM((3 * row, S // 2, C), bf16),
        pltpu.VMEM((2, N, S // 2, B * C), bf16),
        pltpu.VMEM((N, B * C, count * C), bf16),
        pltpu.VMEM((S, count * S), bf16),
        pltpu.VMEM((count, C + 32 * (B - 1), C), f32),
        pltpu.VMEM((N // 2, count * S, 2 * C), bf16),
        pltpu.VMEM((N, S, C), bf16),
        pltpu.VMEM((N, S, C), f32),
        pltpu.VMEM((N, S, C), f32),
        pltpu.VMEM((N, S, B * C), bf16),
        pltpu.VMEM((N, S, B * C), bf16),
        pltpu.VMEM((N, S, C), f32),
        pltpu.VMEM((N, S, S), bf16),
        pltpu.VMEM((N, S, S), bf16),
        pltpu.VMEM((N, B * C, C), bf16),
        pltpu.VMEM((N, B * C, C), bf16),
        pltpu.VMEM((2, row, S, C), bf16),
        pltpu.VMEM((2, row, S, C), bf16),
        pltpu.VMEM((row, S, C), f32),
        pltpu.VMEM((max(X - 1, 1), owned, S, C), bf16),
        pltpu.VMEM((max(X - 1, 1), owned, S, C), bf16),
        dma((2,)),
        dma((N,)),
        dma((N,)),
        dma((2, X, owned)),
        dma((2, X, owned)),
        dma((2, 2, X, owned)),
        dma((2, 2, X, owned)),
        dma((2, B, N)),
        dma((2, B, N)),
        dma((B, N)),
        dma((B, N)),
        dma((B, N)),
        dma((B, N)),
        dma((2, 2, row)),
        dma((2, 2, row)),
        dma((2, max(X - 1, 1), owned)),
        dma((2, max(X - 1, 1), owned)),
    ]
    any_spec = pl.BlockSpec(memory_space=pl.ANY)
    vmem = pl.BlockSpec(memory_space=pltpu.VMEM)
    smem = pl.BlockSpec(memory_space=pltpu.SMEM)
    return pl.pallas_call(
        functools.partial(kernel, (Z, X, B)),
        out_shape=(
            pltpu.VMEM(templates.shape, f32),
            pltpu.VMEM(exposures.shape, f32),
        ),
        in_specs=[any_spec] * 3 + [smem] * 4,
        out_specs=(vmem, vmem),
        scratch_shapes=scratch,
        compiler_params=pltpu.CompilerParams(
            collective_id=0, has_side_effects=True, vmem_limit_bytes=56 * 2**20
        ),
    )(
        templates,
        exposures,
        variance,
        coefficients,
        jnp.swapaxes(psf_width, 2, 3),
        patch_ids,
        live_count,
    )


def solution(mesh):
    in_specs = (
        P(("groups", "exp"), "patch", None, "band"),
        P(("groups", "exp"), "patch", None, None, "band"),
        P(("groups", "exp"), "patch", None, None, "band"),
        P(("groups", "exp"), "patch", None, None),
        P(("groups", "exp"), "patch", None, None),
        P(("groups", "exp"), "patch", None),
        P(("groups", "exp"), "patch"),
    )
    out_specs = (
        P(("groups", "exp"), "patch", None, "band"),
        P(("groups", "exp"), "patch", None, None, "band"),
    )
    return jax.shard_map(
        on_device, mesh=mesh, in_specs=in_specs, out_specs=out_specs, check_vma=False
    )
```

```python
import functools

import jax
import jax.numpy as jnp
import numpy as np
from jax import lax
from jax.experimental import pallas as pl
from jax.experimental.pallas import tpu as pltpu
from jax.sharding import PartitionSpec as P

HW = 10
PW = 7

sigmas = (0.75, 1.5, 3.0)
degrees = (4, 2, 2)
starts = (0, 5, 8)
profiles = [(group, power) for group in range(3) for power in range(degrees[group] + 1)]

MESH = pl.DeviceIdType.MESH


def scale_of(group, power):
    grid = np.arange(-HW, HW + 1).astype(np.float64)
    base = np.exp(-grid * grid / (2.0 * sigmas[group] ** 2)) * (grid / HW) ** power
    return float(1.0 / np.sqrt(np.sum(base * base)))


def profile_tables(offset):
    spot = offset.astype(jnp.float32)
    inside = jnp.abs(offset) <= HW
    ratio = spot * (1.0 / HW)
    tables = []
    for group in range(3):
        value = jnp.exp(spot * spot * (-0.5 / sigmas[group] ** 2))
        value = jnp.where(inside, value, 0.0)
        for power in range(degrees[group] + 1):
            tables.append(value * scale_of(group, power))
            value = value * ratio
    return tables


def point_table(offset, width):
    rate = -0.5 / (width * width)
    total = 1.0 + 2.0 * sum(jnp.exp(rate * float(u * u)) for u in range(1, PW + 1))
    spot = offset.astype(jnp.float32)
    value = jnp.exp(spot * spot * rate) * (1.0 / total)
    return jnp.where(jnp.abs(offset) <= PW, value, 0.0)


def offsets(rows, cols, shift):
    row = lax.broadcasted_iota(jnp.int32, (rows, cols), 0)
    col = lax.broadcasted_iota(jnp.int32, (rows, cols), 1)
    return col - row + shift


def kernel(
    sizes,
    templates,
    exposures,
    variance,
    coeff,
    psf,
    ids,
    live,
    coadd,
    score,
    win0,
    win1,
    tfull,
    mats,
    gcat,
    gtab,
    cols,
    expo,
    inv,
    wval,
    wfull,
    ifull,
    rden,
    prow,
    qrow,
    pcol,
    qcol,
    psend,
    precv,
    pown,
    xsend,
    xrecv,
    local_sem,
    var_sem,
    exp_sem,
    xs_sem,
    xr_sem,
    zs_sem,
    zr_sem,
    ts_sem,
    tr_sem,
    is_sem,
    ir_sem,
    ws_sem,
    wr_sem,
    ps_sem,
    pr_sem,
    ss_sem,
    sr_sem,
    frecv,
    ys_sem,
    yr_sem,
    fs_sem,
    fr_sem,
):
    Z, X, B = sizes
    owned, S, C = templates.shape[1:]
    slots = ids.shape[2]
    N = ids.shape[1] * slots
    row_patches = X * owned
    z = lax.axis_index("exp")
    x = lax.axis_index("patch")
    b = lax.axis_index("band")

    def column(o):
        return lax.rem(x + o, X)

    def back_column(o):
        return lax.rem(x + X - o, X)

    def other_band(o):
        return lax.rem(b + o, B)

    def back_band(o):
        return lax.rem(b + B - o, B)

    to_exists = (z > 0, z < Z - 1)
    from_exists = (z < Z - 1, z > 0)
    target = (z - 1, z + 1)
    lands = (2, 0)

    def remote(src, dst, send, recv, device):
        return pltpu.make_async_remote_copy(
            src_ref=src,
            dst_ref=dst,
            send_sem=send,
            recv_sem=recv,
            device_id=device,
            device_id_type=MESH,
        )

    barrier = pltpu.get_barrier_semaphore()
    for d in range(2):

        @pl.when(to_exists[d])
        def _():
            pl.semaphore_signal(barrier, inc=1, device_id={"exp": target[d]}, device_id_type=MESH)

    for o in range(1, X):
        pl.semaphore_signal(barrier, inc=1, device_id={"patch": column(o)}, device_id_type=MESH)
    for o in range(1, B):
        pl.semaphore_signal(barrier, inc=1, device_id={"band": other_band(o)}, device_id_type=MESH)

    H = S // 2
    win = (win0, win1)
    gs = max(owned // 2, 1)
    groups = owned // gs
    bounds = ((0, H - 16), (H - 16, S))
    relayed = groups > 1 and X > 1
    near = owned - gs if relayed else owned

    def turns(h, i):
        return relayed and h == 0 and i == groups - 1


    def var_copy(n):
        return pltpu.make_async_copy(
            variance.at[0, n // slots, lax.rem(n, slots)], inv.at[n], var_sem.at[n]
        )

    def exp_copy(n):
        return pltpu.make_async_copy(
            exposures.at[0, n // slots, lax.rem(n, slots)], expo.at[n], exp_sem.at[n]
        )

    def own_copy(h):
        return pltpu.make_async_copy(
            templates.at[0, :, pl.ds(h * H, H)],
            win[h].at[pl.ds(row_patches + x * owned, owned)],
            local_sem.at[h],
        )

    def start_local(n, carry):
        var_copy(n).start()
        return carry

    lax.fori_loop(0, N, start_local, 0)
    pl.semaphore_wait(
        barrier,
        (z > 0).astype(jnp.int32) + (z < Z - 1).astype(jnp.int32) + (X - 1) + (B - 1),
    )

    def block(h, i):
        return templates.at[0, pl.ds(i * gs, gs), pl.ds(h * H, H)]

    def place(h, row, o, i):
        return win[h].at[pl.ds(row * row_patches + column(o) * owned + i * gs, gs)]

    def x_copy(h, o, i):
        return remote(
            block(h, i),
            place(h, 1, 0, i),
            xs_sem.at[h, o, i],
            xr_sem.at[h, o, i],
            {"patch": back_column(o)},
        )

    def z_copy(h, d, o, i):
        return remote(
            block(h, i) if o == 0 else place(h, 1, o, i),
            place(h, lands[d], o, i),
            zs_sem.at[h, d, o, i],
            zr_sem.at[h, d, o, i],
            {"exp": target[d]},
        )

    def y_copy(d, o):
        part = place(0, lands[d], 0, groups - 1)
        return remote(part, part, ys_sem.at[d, o], yr_sem.at[d, o], {"patch": back_column(o)})

    def launch_x(h):
        for i in range(groups):
            for o in range(1, X):
                x_copy(h, o, i).start()

    def launch_z(h):
        for i in reversed(range(groups)):
            for d in range(2):

                @pl.when(to_exists[d])
                def _():
                    z_copy(h, d, 0, i).start()

    def forward(h):
        for i in range(groups):
            for o in range(1, X):
                x_copy(h, o, i).wait_recv()
                if turns(h, i):
                    continue
                for d in range(2):

                    @pl.when(to_exists[d])
                    def _():
                        z_copy(h, d, o, i).start()

    def relay():
        if not relayed:
            return
        for d in range(2):

            @pl.when(from_exists[d])
            def _():
                z_copy(0, d, 0, groups - 1).wait_recv()
                for o in range(1, X):
                    y_copy(d, o).start()

    def half_copy(buffer, send, recv, o, n):
        return remote(
            buffer.at[n, :, 0:C],
            buffer.at[n, :, o * C : (o + 1) * C],
            send.at[o, n],
            recv.at[o, n],
            {"band": back_band(o)},
        )

    def invert(n, carry):
        var_copy(n).wait()
        weight = 1.0 / inv[n]
        inv[n] = weight
        ifull[n, :, 0:C] = weight.astype(jnp.bfloat16)
        for o in range(1, B):
            half_copy(ifull, is_sem, ir_sem, o, n).start()
        return carry

    launch_x(0)
    launch_z(0)

    def start_exposure(n, carry):
        exp_copy(n).start()
        return carry

    lax.fori_loop(0, N, start_exposure, 0)
    for h in range(2):
        own_copy(h).start()
    lax.fori_loop(0, N, invert, 0)
    forward(0)
    launch_z(1)
    relay()
    launch_x(1)

    count = len(profiles)
    gcat[...] = jnp.zeros((S, 2 * count * H), jnp.bfloat16)
    for p, table in enumerate(profile_tables(-offsets(H, H, 0))):
        table = table.astype(jnp.bfloat16)
        gcat[0:H, p * H : (p + 1) * H] = table
        gcat[H:S, (count + p) * H : (count + p + 1) * H] = table
    for p, table in enumerate(profile_tables(-offsets(16, H, -H))):
        gcat[H : H + 16, p * H : (p + 1) * H] = table.astype(jnp.bfloat16)
    for p, table in enumerate(profile_tables(-offsets(16, H, 16))):
        gcat[H - 16 : H, (count + p) * H : (count + p + 1) * H] = table.astype(jnp.bfloat16)
    shifts = [(b - other_band(o)) * C for o in range(B)]
    for p, table in enumerate(profile_tables(offsets(C, C, 0))):
        gtab[p, 0:C, :] = table
    for o in range(1, B):
        start = C + (o - 1) * 32
        for p, table in enumerate(profile_tables(offsets(16, C, shifts[o]))):
            gtab[p, start : start + 16, :] = table
        for p, table in enumerate(profile_tables(offsets(16, C, shifts[o] - C + 16))):
            gtab[p, start + 16 : start + 32, :] = table

    def mix(n, carry):
        e, k = n // slots, lax.rem(n, slots)
        if B > 1:
            mats[n, C : B * C, :] = jnp.zeros(((B - 1) * C, count * C), jnp.bfloat16)
        index = 0
        for p, (group, power) in enumerate(profiles):
            value = coeff[0, e, k, index] * gtab[starts[group]]
            index += 1
            for j in range(1, degrees[group] + 1 - power):
                value = value + coeff[0, e, k, index] * gtab[starts[group] + j]
                index += 1
            value = value.astype(jnp.bfloat16)
            lanes = slice(p * C, (p + 1) * C)
            mats[n, 0:C, lanes] = value[0:C]
            for o in range(1, B):
                start = C + (o - 1) * 32
                mats[n, o * C : o * C + 16, lanes] = value[start : start + 16]
                mats[n, (o + 1) * C - 16 : (o + 1) * C, lanes] = value[start + 16 : start + 32]
        return carry

    lax.fori_loop(0, N, mix, 0)
    forward(1)

    for d in range(2):

        @pl.when(jnp.logical_not(from_exists[d]))
        def _():
            for h in range(2):

                def clear(i, carry):
                    win[h][lands[d] * row_patches + i] = jnp.zeros((H, C), jnp.bfloat16)
                    return carry

                lax.fori_loop(0, row_patches, clear, 0)

    def spread(n, carry):
        e, k = n // slots, lax.rem(n, slots)

        def put(low, square, rows, lanes, table):
            low[n, rows, lanes] = table.astype(jnp.bfloat16)
            square[n, rows, lanes] = (table * table).astype(jnp.bfloat16)

        width = jnp.full((1, H), psf[0, e, 0, k], jnp.float32)
        prow[n] = jnp.zeros((S, S), jnp.bfloat16)
        qrow[n] = jnp.zeros((S, S), jnp.bfloat16)
        table = point_table(offsets(H, H, 0), width)
        put(prow, qrow, slice(0, H), slice(0, H), table)
        put(prow, qrow, slice(H, S), slice(H, S), table)
        put(prow, qrow, slice(H, H + 16), slice(0, H), point_table(offsets(16, H, -H), width))
        put(prow, qrow, slice(H - 16, H), slice(H, S), point_table(offsets(16, H, 16), width))
        width = jnp.full((1, C), psf[0, e, 1, k], jnp.float32)
        pcol[n] = jnp.zeros((B * C, C), jnp.bfloat16)
        qcol[n] = jnp.zeros((B * C, C), jnp.bfloat16)
        lanes = slice(0, C)
        put(pcol, qcol, slice(0, C), lanes, point_table(offsets(C, C, 0), width))
        for o in range(1, B):
            first, last = o * C, (o + 1) * C
            table = point_table(offsets(16, C, shifts[o]), width)
            put(pcol, qcol, slice(first, first + 16), lanes, table)
            table = point_table(offsets(16, C, shifts[o] - C + 16), width)
            put(pcol, qcol, slice(last - 16, last), lanes, table)
        return carry

    def alive_of(n):
        e, k = n // slots, lax.rem(n, slots)
        return jnp.where(k < live[0, e], 1.0, 0.0).astype(jnp.float32)

    def matched(chains):
        middle = [
            jnp.dot(rows, full, preferred_element_type=jnp.float32).astype(jnp.bfloat16)
            for rows, full, _ in chains
        ]
        return [
            jnp.dot(part, chain[2], preferred_element_type=jnp.float32)
            for part, chain in zip(middle, chains)
        ]

    def denominator(step, carry):
        tiles = [step * 4 + a for a in range(4)]
        for n in tiles:
            for o in range(1, B):
                half_copy(ifull, is_sem, ir_sem, o, n).wait_recv()
        results = matched([(qrow[n], ifull[n], qcol[n]) for n in tiles])
        for n, result in zip(tiles, results):
            rden[n] = lax.rsqrt(result) * alive_of(n)
        return carry

    def arrive(h):
        own_copy(h).wait()
        for d in range(2):

            @pl.when(from_exists[d])
            def _():
                for o in range(X):
                    for i in range(groups):
                        if not turns(h, i):
                            z_copy(h, d, o, i).wait_recv()
                        elif o > 0:
                            y_copy(d, o).wait_recv()

    def tile_copy(h, o, n):
        return remote(
            tfull.at[h, n, :, 0:C],
            tfull.at[h, n, :, o * C : (o + 1) * C],
            ts_sem.at[h, o, n],
            tr_sem.at[h, o, n],
            {"band": back_band(o)},
        )

    def middle(h):
        first, last = bounds[h]
        depth = (h + 1) * count * H

        def choose(n, carry):
            tfull[h, n, :, 0:C] = win[h][ids[0, n // slots, lax.rem(n, slots)]]
            for o in range(1, B):
                tile_copy(h, o, n).start()
            return carry

        for n in range(N):
            choose(n, 0)
        for n in range(N):
            if h == 0:
                exp_copy(n).wait()
            for o in range(1, B):
                tile_copy(h, o, n).wait_recv()
            tile = tfull[h, n]
            pair, a = n // 2, n % 2
            for p in range(0, count, 2):
                wide = min(2, count - p)
                part = jnp.dot(
                    tile,
                    mats[n, :, p * C : (p + wide) * C],
                    preferred_element_type=jnp.float32,
                ).astype(jnp.bfloat16)
                for v in range(wide):
                    row = (h * count + p + v) * H
                    cols[pair, row : row + H, a * C : (a + 1) * C] = part[:, v * C : (v + 1) * C]
        for pair in range(N // 2):
            convolved = jnp.dot(
                gcat[first:last, 0:depth],
                cols[pair, 0:depth, :],
                preferred_element_type=jnp.float32,
            )
            for a in range(2):
                n = pair * 2 + a
                value = expo[n, first:last, :].astype(jnp.float32)
                value = (value - convolved[:, a * C : (a + 1) * C]) * inv[n, first:last, :]
                wval[n, first:last, :] = value
                wfull[n, first:last, 0:C] = value.astype(jnp.bfloat16)
                if h == 1:
                    for o in range(1, B):
                        half_copy(wfull, ws_sem, wr_sem, o, n).start()

    def partials(h, q, rows):
        first, last = bounds[h]
        factors = []
        for row in rows:
            hits = []
            for n in range(N):
                e, k = n // slots, n % slots
                hit = jnp.logical_and(ids[0, e, k] == row * row_patches + q, k < live[0, e])
                hits.append(jnp.where(hit, 1.0, 0.0).astype(jnp.float32))
            factors.append(hits)
        step = 16
        for start in range(first, last, step):
            values = [jnp.zeros((step, C), jnp.float32) for _ in rows]
            for n in range(N):
                tile = wval[n, start : start + step, :]
                values = [value + hits[n] * tile for value, hits in zip(values, factors)]
            yield slice(start, start + step), values

    def p_copy(h, d, q, t):
        first, last = bounds[h]
        rows = pl.ds(first, last - first)
        return remote(
            psend.at[d, q, rows],
            precv.at[d, q, rows],
            ps_sem.at[h, d, t],
            pr_sem.at[h, d, t],
            {"exp": target[d]},
        )

    def f_copy(d, s, i):
        first, last = bounds[0]
        rows = pl.ds(first, last - first)
        return remote(
            psend.at[d, column(s + 1) * owned + i, rows],
            frecv.at[d, s, i - near, rows],
            fs_sem.at[d, s, i - near],
            fr_sem.at[d, s, i - near],
            {"patch": column(s + 1)},
        )

    def push(h):
        first, last = bounds[h]
        limit = near if h == 0 else owned

        def fill(q):
            for rows, (up, own, down) in partials(h, q, (0, 1, 2)):
                psend[0, q, rows, :] = up.astype(jnp.bfloat16)
                psend[1, q, rows, :] = down.astype(jnp.bfloat16)
                pown[q, rows, :] = own

        def along(t, carry):
            s, i = t // gs, near + lax.rem(t, gs)
            fill(column(s + 1) * owned + i)
            for d in range(2):

                @pl.when(to_exists[d])
                def _():
                    f_copy(d, s, i).start()

            return carry

        def step(t, carry):
            s, i = t // limit, lax.rem(t, limit)
            q = column(s + 1) * owned + i
            fill(q)
            for d in range(2):

                @pl.when(to_exists[d])
                def _():
                    p_copy(h, d, q, s * owned + i).start()

            return carry

        def joined(i, carry):
            q = x * owned + i
            fill(q)
            for d in range(2):

                @pl.when(to_exists[d])
                def _():
                    value = psend[d, q, first:last, :].astype(jnp.float32)
                    for s in range(X - 1):
                        f_copy(d, s, i).wait_recv()
                        value = value + frecv[d, s, i - near, first:last, :].astype(jnp.float32)
                    psend[d, q, first:last, :] = value.astype(jnp.bfloat16)
                    p_copy(h, d, q, (X - 1) * owned + i).start()

            return carry

        if limit < owned:
            lax.fori_loop(0, (X - 1) * gs, along, 0)
        lax.fori_loop(0, X * limit, step, 0)
        if limit < owned:
            lax.fori_loop(limit, owned, joined, 0)

    def numerator(step, carry):
        tiles = [step * 4 + a for a in range(4)]
        for n in tiles:
            for o in range(1, B):
                half_copy(wfull, ws_sem, wr_sem, o, n).wait_recv()
        results = matched([(prow[n], wfull[n], pcol[n]) for n in tiles])
        for n, result in zip(tiles, results):
            score[0, n // slots, lax.rem(n, slots)] = result * rden[n]
        return carry

    def gather_rows(h, t, q):
        first, last = bounds[h]
        for d in range(2):

            @pl.when(from_exists[d])
            def _():
                p_copy(h, d, q, t).wait_recv()
                pown[q, first:last, :] += precv[d, q, first:last, :].astype(jnp.float32)

    def s_copy(h, s, i):
        first, last = bounds[h]
        rows = pl.ds(first, last - first)
        return remote(
            xsend.at[s, i, rows],
            xrecv.at[s, i, rows],
            ss_sem.at[h, s, i],
            sr_sem.at[h, s, i],
            {"patch": column(s + 1)},
        )

    def pass_on(h):
        first, last = bounds[h]
        for s in range(X - 1):
            for i in range(owned):
                q = column(s + 1) * owned + i
                if h == 1 or i < near:
                    gather_rows(h, s * owned + i, q)
                xsend[s, i, first:last, :] = pown[q, first:last, :].astype(jnp.bfloat16)
                s_copy(h, s, i).start()

    def finish_sums(h):
        first, last = bounds[h]
        for i in range(owned):
            q = x * owned + i
            gather_rows(h, (X - 1) * owned + i, q)
            value = pown[q, first:last, :]
            for s in range(X - 1):
                s_copy(h, s, i).wait_recv()
                value = value + xrecv[s, i, first:last, :].astype(jnp.float32)
            coadd[0, i, first:last, :] = value

    arrive(0)
    middle(0)
    push(0)
    arrive(1)
    middle(1)
    push(1)
    pass_on(0)
    lax.fori_loop(0, N, spread, 0)
    lax.fori_loop(0, N // 4, denominator, 0)
    pass_on(1)
    finish_sums(0)
    lax.fori_loop(0, N // 4, numerator, 0)
    finish_sums(1)

    for h in range(2):
        for o in range(1, X):
            for i in range(groups):
                x_copy(h, o, i).wait_send()
            for i in range(owned):
                s_copy(h, o - 1, i).wait_send()
        for d in range(2):

            @pl.when(to_exists[d])
            def _():
                for o in range(X):
                    for i in range(groups):
                        if o == 0 or not turns(h, i):
                            z_copy(h, d, o, i).wait_send()
                for s in range(X):
                    for i in range(owned):
                        if h == 1 or s == X - 1 or i < near:
                            p_copy(h, d, column(s + 1) * owned + i, s * owned + i).wait_send()
                        else:
                            f_copy(d, s, i).wait_send()

            if relayed and h == 0:

                @pl.when(from_exists[d])
                def _():
                    for o in range(1, X):
                        y_copy(d, o).wait_send()

    def finish(n, carry):
        for o in range(1, B):
            half_copy(ifull, is_sem, ir_sem, o, n).wait_send()
            half_copy(wfull, ws_sem, wr_sem, o, n).wait_send()
            for h in range(2):
                tile_copy(h, o, n).wait_send()
        return carry

    lax.fori_loop(0, N, finish, 0)


def on_device(templates, exposures, variance, coefficients, psf_width, patch_ids, live_count):
    owned, S, C = templates.shape[1:]
    Z, X, B = (lax.axis_size(axis) for axis in ("exp", "patch", "band"))
    N = patch_ids.shape[1] * patch_ids.shape[2]
    row = X * owned
    count = len(profiles)
    bf16, f32 = jnp.bfloat16, jnp.float32
    dma = pltpu.SemaphoreType.DMA
    scratch = [
        pltpu.VMEM((3 * row, S // 2, C), bf16),
        pltpu.VMEM((3 * row, S // 2, C), bf16),
        pltpu.VMEM((2, N, S // 2, B * C), bf16),
        pltpu.VMEM((N, B * C, count * C), bf16),
        pltpu.VMEM((S, count * S), bf16),
        pltpu.VMEM((count, C + 32 * (B - 1), C), f32),
        pltpu.VMEM((N // 2, count * S, 2 * C), bf16),
        pltpu.VMEM((N, S, C), bf16),
        pltpu.VMEM((N, S, C), f32),
        pltpu.VMEM((N, S, C), f32),
        pltpu.VMEM((N, S, B * C), bf16),
        pltpu.VMEM((N, S, B * C), bf16),
        pltpu.VMEM((N, S, C), f32),
        pltpu.VMEM((N, S, S), bf16),
        pltpu.VMEM((N, S, S), bf16),
        pltpu.VMEM((N, B * C, C), bf16),
        pltpu.VMEM((N, B * C, C), bf16),
        pltpu.VMEM((2, row, S, C), bf16),
        pltpu.VMEM((2, row, S, C), bf16),
        pltpu.VMEM((row, S, C), f32),
        pltpu.VMEM((max(X - 1, 1), owned, S, C), bf16),
        pltpu.VMEM((max(X - 1, 1), owned, S, C), bf16),
        dma((2,)),
        dma((N,)),
        dma((N,)),
        dma((2, X, owned)),
        dma((2, X, owned)),
        dma((2, 2, X, owned)),
        dma((2, 2, X, owned)),
        dma((2, B, N)),
        dma((2, B, N)),
        dma((B, N)),
        dma((B, N)),
        dma((B, N)),
        dma((B, N)),
        dma((2, 2, row)),
        dma((2, 2, row)),
        dma((2, max(X - 1, 1), owned)),
        dma((2, max(X - 1, 1), owned)),
        pltpu.VMEM((2, max(X - 1, 1), max(owned // 2, 1), S, C), bf16),
        dma((2, X)),
        dma((2, X)),
        dma((2, max(X - 1, 1), max(owned // 2, 1))),
        dma((2, max(X - 1, 1), max(owned // 2, 1))),
    ]
    any_spec = pl.BlockSpec(memory_space=pl.ANY)
    vmem = pl.BlockSpec(memory_space=pltpu.VMEM)
    smem = pl.BlockSpec(memory_space=pltpu.SMEM)
    return pl.pallas_call(
        functools.partial(kernel, (Z, X, B)),
        out_shape=(
            pltpu.VMEM(templates.shape, f32),
            pltpu.VMEM(exposures.shape, f32),
        ),
        in_specs=[any_spec] * 3 + [smem] * 4,
        out_specs=(vmem, vmem),
        scratch_shapes=scratch,
        compiler_params=pltpu.CompilerParams(
            collective_id=0, has_side_effects=True, vmem_limit_bytes=56 * 2**20
        ),
    )(
        templates,
        exposures,
        variance,
        coefficients,
        jnp.swapaxes(psf_width, 2, 3),
        patch_ids,
        live_count,
    )


def solution(mesh):
    in_specs = (
        P(("groups", "exp"), "patch", None, "band"),
        P(("groups", "exp"), "patch", None, None, "band"),
        P(("groups", "exp"), "patch", None, None, "band"),
        P(("groups", "exp"), "patch", None, None),
        P(("groups", "exp"), "patch", None, None),
        P(("groups", "exp"), "patch", None),
        P(("groups", "exp"), "patch"),
    )
    out_specs = (
        P(("groups", "exp"), "patch", None, "band"),
        P(("groups", "exp"), "patch", None, None, "band"),
    )
    return jax.shard_map(
        on_device, mesh=mesh, in_specs=in_specs, out_specs=out_specs, check_vma=False
    )
```

```python
import functools

import jax
import jax.numpy as jnp
import numpy as np
from jax import lax
from jax.experimental import pallas as pl
from jax.experimental.pallas import tpu as pltpu
from jax.sharding import PartitionSpec as P

HW = 10
PW = 7

sigmas = (0.75, 1.5, 3.0)
degrees = (4, 2, 2)
starts = (0, 5, 8)
profiles = [(group, power) for group in range(3) for power in range(degrees[group] + 1)]

MESH = pl.DeviceIdType.MESH


def scale_of(group, power):
    grid = np.arange(-HW, HW + 1).astype(np.float64)
    base = np.exp(-grid * grid / (2.0 * sigmas[group] ** 2)) * (grid / HW) ** power
    return float(1.0 / np.sqrt(np.sum(base * base)))


def profile_tables(offset):
    spot = offset.astype(jnp.float32)
    inside = jnp.abs(offset) <= HW
    ratio = spot * (1.0 / HW)
    tables = []
    for group in range(3):
        value = jnp.exp(spot * spot * (-0.5 / sigmas[group] ** 2))
        value = jnp.where(inside, value, 0.0)
        for power in range(degrees[group] + 1):
            tables.append(value * scale_of(group, power))
            value = value * ratio
    return tables


def point_table(offset, width):
    rate = -0.5 / (width * width)
    total = 1.0 + 2.0 * sum(jnp.exp(rate * float(u * u)) for u in range(1, PW + 1))
    spot = offset.astype(jnp.float32)
    value = jnp.exp(spot * spot * rate) * (1.0 / total)
    return jnp.where(jnp.abs(offset) <= PW, value, 0.0)


def offsets(rows, cols, shift):
    row = lax.broadcasted_iota(jnp.int32, (rows, cols), 0)
    col = lax.broadcasted_iota(jnp.int32, (rows, cols), 1)
    return col - row + shift


def kernel(
    sizes,
    templates,
    exposures,
    variance,
    coeff,
    psf,
    ids,
    live,
    coadd,
    score,
    win0,
    win1,
    tfull,
    mats,
    gcat,
    gtab,
    cols,
    expo,
    inv,
    wval,
    wfull,
    ifull,
    rden,
    prow,
    qrow,
    pcol,
    qcol,
    psend,
    precv,
    pown,
    xsend,
    xrecv,
    local_sem,
    var_sem,
    exp_sem,
    xs_sem,
    xr_sem,
    zs_sem,
    zr_sem,
    ts_sem,
    tr_sem,
    is_sem,
    ir_sem,
    ws_sem,
    wr_sem,
    ps_sem,
    pr_sem,
    ss_sem,
    sr_sem,
):
    Z, X, B = sizes
    owned, S, C = templates.shape[1:]
    slots = ids.shape[2]
    N = ids.shape[1] * slots
    row_patches = X * owned
    z = lax.axis_index("exp")
    x = lax.axis_index("patch")
    b = lax.axis_index("band")

    def column(o):
        return lax.rem(x + o, X)

    def back_column(o):
        return lax.rem(x + X - o, X)

    def other_band(o):
        return lax.rem(b + o, B)

    def back_band(o):
        return lax.rem(b + B - o, B)

    to_exists = (z > 0, z < Z - 1)
    from_exists = (z < Z - 1, z > 0)
    target = (z - 1, z + 1)
    lands = (2, 0)

    def remote(src, dst, send, recv, device):
        return pltpu.make_async_remote_copy(
            src_ref=src,
            dst_ref=dst,
            send_sem=send,
            recv_sem=recv,
            device_id=device,
            device_id_type=MESH,
        )

    barrier = pltpu.get_barrier_semaphore()
    for d in range(2):

        @pl.when(to_exists[d])
        def _():
            pl.semaphore_signal(barrier, inc=1, device_id={"exp": target[d]}, device_id_type=MESH)

    for o in range(1, X):
        pl.semaphore_signal(barrier, inc=1, device_id={"patch": column(o)}, device_id_type=MESH)
    for o in range(1, B):
        pl.semaphore_signal(barrier, inc=1, device_id={"band": other_band(o)}, device_id_type=MESH)

    H = S // 2
    win = (win0, win1)
    gs = max(owned // 2, 1)
    groups = owned // gs
    bounds = ((0, H - 16), (H - 16, S))

    def var_copy(n):
        return pltpu.make_async_copy(
            variance.at[0, n // slots, lax.rem(n, slots)], inv.at[n], var_sem.at[n]
        )

    def exp_copy(n):
        return pltpu.make_async_copy(
            exposures.at[0, n // slots, lax.rem(n, slots)], expo.at[n], exp_sem.at[n]
        )

    def own_copy(h):
        return pltpu.make_async_copy(
            templates.at[0, :, pl.ds(h * H, H)],
            win[h].at[pl.ds(row_patches + x * owned, owned)],
            local_sem.at[h],
        )

    def start_local(n, carry):
        var_copy(n).start()
        return carry

    lax.fori_loop(0, N, start_local, 0)
    pl.semaphore_wait(
        barrier,
        (z > 0).astype(jnp.int32) + (z < Z - 1).astype(jnp.int32) + (X - 1) + (B - 1),
    )

    def block(h, i):
        return templates.at[0, pl.ds(i * gs, gs), pl.ds(h * H, H)]

    def place(h, row, o, i):
        return win[h].at[pl.ds(row * row_patches + column(o) * owned + i * gs, gs)]

    def x_copy(h, o, i):
        return remote(
            block(h, i),
            place(h, 1, 0, i),
            xs_sem.at[h, o, i],
            xr_sem.at[h, o, i],
            {"patch": back_column(o)},
        )

    def z_copy(h, d, o, i):
        return remote(
            block(h, i) if o == 0 else place(h, 1, o, i),
            place(h, lands[d], o, i),
            zs_sem.at[h, d, o, i],
            zr_sem.at[h, d, o, i],
            {"exp": target[d]},
        )

    def launch_x(h):
        for i in range(groups):
            for o in range(1, X):
                x_copy(h, o, i).start()

    def launch_z(h):
        for i in range(groups):
            for d in range(2):

                @pl.when(to_exists[d])
                def _():
                    z_copy(h, d, 0, i).start()

    def forward(h):
        for i in range(groups):
            for o in range(1, X):
                x_copy(h, o, i).wait_recv()
                for d in range(2):

                    @pl.when(to_exists[d])
                    def _():
                        z_copy(h, d, o, i).start()

    def half_copy(buffer, send, recv, o, n):
        return remote(
            buffer.at[n, :, 0:C],
            buffer.at[n, :, o * C : (o + 1) * C],
            send.at[o, n],
            recv.at[o, n],
            {"band": back_band(o)},
        )

    def invert(n, carry):
        var_copy(n).wait()
        weight = 1.0 / inv[n]
        inv[n] = weight
        ifull[n, :, 0:C] = weight.astype(jnp.bfloat16)
        for o in range(1, B):
            half_copy(ifull, is_sem, ir_sem, o, n).start()
        return carry

    launch_x(0)
    launch_z(0)
    launch_x(1)

    def start_exposure(n, carry):
        exp_copy(n).start()
        return carry

    lax.fori_loop(0, N, start_exposure, 0)
    for h in range(2):
        own_copy(h).start()
    lax.fori_loop(0, N // 2, invert, 0)
    forward(0)
    launch_z(1)
    lax.fori_loop(N // 2, N, invert, 0)

    count = len(profiles)
    gcat[...] = jnp.zeros((S, 2 * count * H), jnp.bfloat16)
    for p, table in enumerate(profile_tables(-offsets(H, H, 0))):
        table = table.astype(jnp.bfloat16)
        gcat[0:H, p * H : (p + 1) * H] = table
        gcat[H:S, (count + p) * H : (count + p + 1) * H] = table
    for p, table in enumerate(profile_tables(-offsets(16, H, -H))):
        gcat[H : H + 16, p * H : (p + 1) * H] = table.astype(jnp.bfloat16)
    for p, table in enumerate(profile_tables(-offsets(16, H, 16))):
        gcat[H - 16 : H, (count + p) * H : (count + p + 1) * H] = table.astype(jnp.bfloat16)
    shifts = [(b - other_band(o)) * C for o in range(B)]
    for p, table in enumerate(profile_tables(offsets(C, C, 0))):
        gtab[p, 0:C, :] = table
    for o in range(1, B):
        start = C + (o - 1) * 32
        for p, table in enumerate(profile_tables(offsets(16, C, shifts[o]))):
            gtab[p, start : start + 16, :] = table
        for p, table in enumerate(profile_tables(offsets(16, C, shifts[o] - C + 16))):
            gtab[p, start + 16 : start + 32, :] = table

    def mix(n, carry):
        e, k = n // slots, lax.rem(n, slots)
        if B > 1:
            mats[n, C : B * C, :] = jnp.zeros(((B - 1) * C, count * C), jnp.bfloat16)
        index = 0
        for p, (group, power) in enumerate(profiles):
            value = coeff[0, e, k, index] * gtab[starts[group]]
            index += 1
            for j in range(1, degrees[group] + 1 - power):
                value = value + coeff[0, e, k, index] * gtab[starts[group] + j]
                index += 1
            value = value.astype(jnp.bfloat16)
            lanes = slice(p * C, (p + 1) * C)
            mats[n, 0:C, lanes] = value[0:C]
            for o in range(1, B):
                start = C + (o - 1) * 32
                mats[n, o * C : o * C + 16, lanes] = value[start : start + 16]
                mats[n, (o + 1) * C - 16 : (o + 1) * C, lanes] = value[start + 16 : start + 32]
        return carry

    forward(1)
    lax.fori_loop(0, N, mix, 0)

    for d in range(2):

        @pl.when(jnp.logical_not(from_exists[d]))
        def _():
            for h in range(2):

                def clear(i, carry):
                    win[h][lands[d] * row_patches + i] = jnp.zeros((H, C), jnp.bfloat16)
                    return carry

                lax.fori_loop(0, row_patches, clear, 0)

    def spread(n, carry):
        e, k = n // slots, lax.rem(n, slots)

        def put(low, square, rows, lanes, table):
            low[n, rows, lanes] = table.astype(jnp.bfloat16)
            square[n, rows, lanes] = (table * table).astype(jnp.bfloat16)

        width = jnp.full((1, H), psf[0, e, 0, k], jnp.float32)
        prow[n] = jnp.zeros((S, S), jnp.bfloat16)
        qrow[n] = jnp.zeros((S, S), jnp.bfloat16)
        table = point_table(offsets(H, H, 0), width)
        put(prow, qrow, slice(0, H), slice(0, H), table)
        put(prow, qrow, slice(H, S), slice(H, S), table)
        put(prow, qrow, slice(H, H + 16), slice(0, H), point_table(offsets(16, H, -H), width))
        put(prow, qrow, slice(H - 16, H), slice(H, S), point_table(offsets(16, H, 16), width))
        width = jnp.full((1, C), psf[0, e, 1, k], jnp.float32)
        pcol[n] = jnp.zeros((B * C, C), jnp.bfloat16)
        qcol[n] = jnp.zeros((B * C, C), jnp.bfloat16)
        lanes = slice(0, C)
        put(pcol, qcol, slice(0, C), lanes, point_table(offsets(C, C, 0), width))
        for o in range(1, B):
            first, last = o * C, (o + 1) * C
            table = point_table(offsets(16, C, shifts[o]), width)
            put(pcol, qcol, slice(first, first + 16), lanes, table)
            table = point_table(offsets(16, C, shifts[o] - C + 16), width)
            put(pcol, qcol, slice(last - 16, last), lanes, table)
        return carry

    def alive_of(n):
        e, k = n // slots, lax.rem(n, slots)
        return jnp.where(k < live[0, e], 1.0, 0.0).astype(jnp.float32)

    def matched(chains):
        middle = [
            jnp.dot(rows, full, preferred_element_type=jnp.float32).astype(jnp.bfloat16)
            for rows, full, _ in chains
        ]
        return [
            jnp.dot(part, chain[2], preferred_element_type=jnp.float32)
            for part, chain in zip(middle, chains)
        ]

    def denominator(step, carry):
        tiles = [step * 4 + a for a in range(4)]
        for n in tiles:
            for o in range(1, B):
                half_copy(ifull, is_sem, ir_sem, o, n).wait_recv()
        results = matched([(qrow[n], ifull[n], qcol[n]) for n in tiles])
        for n, result in zip(tiles, results):
            rden[n] = lax.rsqrt(result) * alive_of(n)
        return carry

    def arrive(h):
        own_copy(h).wait()
        for d in range(2):

            @pl.when(from_exists[d])
            def _():
                for o in range(X):
                    for i in range(groups):
                        z_copy(h, d, o, i).wait_recv()

    def tile_copy(h, o, n):
        return remote(
            tfull.at[h, n, :, 0:C],
            tfull.at[h, n, :, o * C : (o + 1) * C],
            ts_sem.at[h, o, n],
            tr_sem.at[h, o, n],
            {"band": back_band(o)},
        )

    def middle(h):
        first, last = bounds[h]
        depth = (h + 1) * count * H

        def choose(n, carry):
            tfull[h, n, :, 0:C] = win[h][ids[0, n // slots, lax.rem(n, slots)]]
            for o in range(1, B):
                tile_copy(h, o, n).start()
            return carry

        for n in range(N):
            choose(n, 0)
        for n in range(N):
            if h == 0:
                exp_copy(n).wait()
            for o in range(1, B):
                tile_copy(h, o, n).wait_recv()
            tile = tfull[h, n]
            pair, a = n // 2, n % 2
            for p in range(0, count, 2):
                wide = min(2, count - p)
                part = jnp.dot(
                    tile,
                    mats[n, :, p * C : (p + wide) * C],
                    preferred_element_type=jnp.float32,
                ).astype(jnp.bfloat16)
                for v in range(wide):
                    row = (h * count + p + v) * H
                    cols[pair, row : row + H, a * C : (a + 1) * C] = part[:, v * C : (v + 1) * C]
        for pair in range(N // 2):
            convolved = jnp.dot(
                gcat[first:last, 0:depth],
                cols[pair, 0:depth, :],
                preferred_element_type=jnp.float32,
            )
            for a in range(2):
                n = pair * 2 + a
                value = expo[n, first:last, :].astype(jnp.float32)
                value = (value - convolved[:, a * C : (a + 1) * C]) * inv[n, first:last, :]
                wval[n, first:last, :] = value
                wfull[n, first:last, 0:C] = value.astype(jnp.bfloat16)
                if h == 1:
                    for o in range(1, B):
                        half_copy(wfull, ws_sem, wr_sem, o, n).start()

    def partials(h, q, rows):
        first, last = bounds[h]
        factors = []
        for row in rows:
            hits = []
            for n in range(N):
                e, k = n // slots, n % slots
                hit = jnp.logical_and(ids[0, e, k] == row * row_patches + q, k < live[0, e])
                hits.append(jnp.where(hit, 1.0, 0.0).astype(jnp.float32))
            factors.append(hits)
        step = 16
        for start in range(first, last, step):
            values = [jnp.zeros((step, C), jnp.float32) for _ in rows]
            for n in range(N):
                tile = wval[n, start : start + step, :]
                values = [value + hits[n] * tile for value, hits in zip(values, factors)]
            yield slice(start, start + step), values

    def p_copy(h, d, q, t):
        first, last = bounds[h]
        rows = pl.ds(first, last - first)
        return remote(
            psend.at[d, q, rows],
            precv.at[d, q, rows],
            ps_sem.at[h, d, t],
            pr_sem.at[h, d, t],
            {"exp": target[d]},
        )

    def patch_of(t):
        return lax.rem(x + 1 + t // owned, X) * owned + lax.rem(t, owned)

    def push(h):
        def step(t, carry):
            q = patch_of(t)
            for rows, (up, own, down) in partials(h, q, (0, 1, 2)):
                psend[0, q, rows, :] = up.astype(jnp.bfloat16)
                psend[1, q, rows, :] = down.astype(jnp.bfloat16)
                pown[q, rows, :] = own
            for d in range(2):

                @pl.when(to_exists[d])
                def _():
                    p_copy(h, d, q, t).start()

            return carry

        lax.fori_loop(0, row_patches, step, 0)

    def numerator(step, carry):
        tiles = [step * 4 + a for a in range(4)]
        for n in tiles:
            for o in range(1, B):
                half_copy(wfull, ws_sem, wr_sem, o, n).wait_recv()
        results = matched([(prow[n], wfull[n], pcol[n]) for n in tiles])
        for n, result in zip(tiles, results):
            score[0, n // slots, lax.rem(n, slots)] = result * rden[n]
        return carry

    def gather_rows(h, t, q):
        first, last = bounds[h]
        for d in range(2):

            @pl.when(from_exists[d])
            def _():
                p_copy(h, d, q, t).wait_recv()
                pown[q, first:last, :] += precv[d, q, first:last, :].astype(jnp.float32)

    def s_copy(h, s, i):
        first, last = bounds[h]
        rows = pl.ds(first, last - first)
        return remote(
            xsend.at[s, i, rows],
            xrecv.at[s, i, rows],
            ss_sem.at[h, s, i],
            sr_sem.at[h, s, i],
            {"patch": column(s + 1)},
        )

    def pass_on(h):
        first, last = bounds[h]
        for s in range(X - 1):
            for i in range(owned):
                q = column(s + 1) * owned + i
                gather_rows(h, s * owned + i, q)
                xsend[s, i, first:last, :] = pown[q, first:last, :].astype(jnp.bfloat16)
                s_copy(h, s, i).start()

    def finish_sums(h):
        first, last = bounds[h]
        for i in range(owned):
            q = x * owned + i
            gather_rows(h, (X - 1) * owned + i, q)
            value = pown[q, first:last, :]
            for s in range(X - 1):
                s_copy(h, s, i).wait_recv()
                value = value + xrecv[s, i, first:last, :].astype(jnp.float32)
            coadd[0, i, first:last, :] = value

    arrive(0)
    middle(0)
    push(0)
    arrive(1)
    middle(1)
    push(1)
    pass_on(0)
    lax.fori_loop(0, N, spread, 0)
    denominator(0, 0)
    pass_on(1)
    lax.fori_loop(1, N // 4, denominator, 0)
    finish_sums(0)
    lax.fori_loop(0, N // 4, numerator, 0)
    finish_sums(1)

    for h in range(2):
        for o in range(1, X):
            for i in range(groups):
                x_copy(h, o, i).wait_send()
            for i in range(owned):
                s_copy(h, o - 1, i).wait_send()
        for d in range(2):

            @pl.when(to_exists[d])
            def _():
                for o in range(X):
                    for i in range(groups):
                        z_copy(h, d, o, i).wait_send()

                def sent(t, carry):
                    p_copy(h, d, patch_of(t), t).wait_send()
                    return carry

                lax.fori_loop(0, row_patches, sent, 0)

    def finish(n, carry):
        for o in range(1, B):
            half_copy(ifull, is_sem, ir_sem, o, n).wait_send()
            half_copy(wfull, ws_sem, wr_sem, o, n).wait_send()
            for h in range(2):
                tile_copy(h, o, n).wait_send()
        return carry

    lax.fori_loop(0, N, finish, 0)


def on_device(templates, exposures, variance, coefficients, psf_width, patch_ids, live_count):
    owned, S, C = templates.shape[1:]
    Z, X, B = (lax.axis_size(axis) for axis in ("exp", "patch", "band"))
    N = patch_ids.shape[1] * patch_ids.shape[2]
    row = X * owned
    count = len(profiles)
    bf16, f32 = jnp.bfloat16, jnp.float32
    dma = pltpu.SemaphoreType.DMA
    scratch = [
        pltpu.VMEM((3 * row, S // 2, C), bf16),
        pltpu.VMEM((3 * row, S // 2, C), bf16),
        pltpu.VMEM((2, N, S // 2, B * C), bf16),
        pltpu.VMEM((N, B * C, count * C), bf16),
        pltpu.VMEM((S, count * S), bf16),
        pltpu.VMEM((count, C + 32 * (B - 1), C), f32),
        pltpu.VMEM((N // 2, count * S, 2 * C), bf16),
        pltpu.VMEM((N, S, C), bf16),
        pltpu.VMEM((N, S, C), f32),
        pltpu.VMEM((N, S, C), f32),
        pltpu.VMEM((N, S, B * C), bf16),
        pltpu.VMEM((N, S, B * C), bf16),
        pltpu.VMEM((N, S, C), f32),
        pltpu.VMEM((N, S, S), bf16),
        pltpu.VMEM((N, S, S), bf16),
        pltpu.VMEM((N, B * C, C), bf16),
        pltpu.VMEM((N, B * C, C), bf16),
        pltpu.VMEM((2, row, S, C), bf16),
        pltpu.VMEM((2, row, S, C), bf16),
        pltpu.VMEM((row, S, C), f32),
        pltpu.VMEM((max(X - 1, 1), owned, S, C), bf16),
        pltpu.VMEM((max(X - 1, 1), owned, S, C), bf16),
        dma((2,)),
        dma((N,)),
        dma((N,)),
        dma((2, X, owned)),
        dma((2, X, owned)),
        dma((2, 2, X, owned)),
        dma((2, 2, X, owned)),
        dma((2, B, N)),
        dma((2, B, N)),
        dma((B, N)),
        dma((B, N)),
        dma((B, N)),
        dma((B, N)),
        dma((2, 2, row)),
        dma((2, 2, row)),
        dma((2, max(X - 1, 1), owned)),
        dma((2, max(X - 1, 1), owned)),
    ]
    any_spec = pl.BlockSpec(memory_space=pl.ANY)
    vmem = pl.BlockSpec(memory_space=pltpu.VMEM)
    smem = pl.BlockSpec(memory_space=pltpu.SMEM)
    return pl.pallas_call(
        functools.partial(kernel, (Z, X, B)),
        out_shape=(
            pltpu.VMEM(templates.shape, f32),
            pltpu.VMEM(exposures.shape, f32),
        ),
        in_specs=[any_spec] * 3 + [smem] * 4,
        out_specs=(vmem, vmem),
        scratch_shapes=scratch,
        compiler_params=pltpu.CompilerParams(
            collective_id=0, has_side_effects=True, vmem_limit_bytes=56 * 2**20
        ),
    )(
        templates,
        exposures,
        variance,
        coefficients,
        jnp.swapaxes(psf_width, 2, 3),
        patch_ids,
        live_count,
    )


def solution(mesh):
    in_specs = (
        P(("groups", "exp"), "patch", None, "band"),
        P(("groups", "exp"), "patch", None, None, "band"),
        P(("groups", "exp"), "patch", None, None, "band"),
        P(("groups", "exp"), "patch", None, None),
        P(("groups", "exp"), "patch", None, None),
        P(("groups", "exp"), "patch", None),
        P(("groups", "exp"), "patch"),
    )
    out_specs = (
        P(("groups", "exp"), "patch", None, "band"),
        P(("groups", "exp"), "patch", None, None, "band"),
    )
    return jax.shard_map(
        on_device, mesh=mesh, in_specs=in_specs, out_specs=out_specs, check_vma=False
    )
```

```python
import functools

import jax
import jax.numpy as jnp
import numpy as np
from jax import lax
from jax.experimental import pallas as pl
from jax.experimental.pallas import tpu as pltpu
from jax.sharding import PartitionSpec as P

HW = 10
PW = 7

sigmas = (0.75, 1.5, 3.0)
degrees = (4, 2, 2)
starts = (0, 5, 8)
profiles = [(group, power) for group in range(3) for power in range(degrees[group] + 1)]

MESH = pl.DeviceIdType.MESH


def scale_of(group, power):
    grid = np.arange(-HW, HW + 1).astype(np.float64)
    base = np.exp(-grid * grid / (2.0 * sigmas[group] ** 2)) * (grid / HW) ** power
    return float(1.0 / np.sqrt(np.sum(base * base)))


def profile_tables(offset):
    spot = offset.astype(jnp.float32)
    inside = jnp.abs(offset) <= HW
    ratio = spot * (1.0 / HW)
    tables = []
    for group in range(3):
        value = jnp.exp(spot * spot * (-0.5 / sigmas[group] ** 2))
        value = jnp.where(inside, value, 0.0)
        for power in range(degrees[group] + 1):
            tables.append(value * scale_of(group, power))
            value = value * ratio
    return tables


def point_table(offset, width):
    rate = -0.5 / (width * width)
    total = 1.0 + 2.0 * sum(jnp.exp(rate * float(u * u)) for u in range(1, PW + 1))
    spot = offset.astype(jnp.float32)
    value = jnp.exp(spot * spot * rate) * (1.0 / total)
    return jnp.where(jnp.abs(offset) <= PW, value, 0.0)


def offsets(rows, cols, shift):
    row = lax.broadcasted_iota(jnp.int32, (rows, cols), 0)
    col = lax.broadcasted_iota(jnp.int32, (rows, cols), 1)
    return col - row + shift


def kernel(
    sizes,
    templates,
    exposures,
    variance,
    coeff,
    psf,
    ids,
    live,
    coadd,
    score,
    win0,
    win1,
    tfull,
    mats,
    gcat,
    gtab,
    cols,
    expo,
    inv,
    wval,
    wfull,
    ifull,
    rden,
    prow,
    qrow,
    pcol,
    qcol,
    psend,
    precv,
    pown,
    xsend,
    xrecv,
    local_sem,
    var_sem,
    exp_sem,
    xs_sem,
    xr_sem,
    zs_sem,
    zr_sem,
    ts_sem,
    tr_sem,
    is_sem,
    ir_sem,
    ws_sem,
    wr_sem,
    ps_sem,
    pr_sem,
    ss_sem,
    sr_sem,
):
    Z, X, B = sizes
    owned, S, C = templates.shape[1:]
    slots = ids.shape[2]
    N = ids.shape[1] * slots
    row_patches = X * owned
    z = lax.axis_index("exp")
    x = lax.axis_index("patch")
    b = lax.axis_index("band")

    def column(o):
        return lax.rem(x + o, X)

    def back_column(o):
        return lax.rem(x + X - o, X)

    def other_band(o):
        return lax.rem(b + o, B)

    def back_band(o):
        return lax.rem(b + B - o, B)

    to_exists = (z > 0, z < Z - 1)
    from_exists = (z < Z - 1, z > 0)
    target = (z - 1, z + 1)
    lands = (2, 0)

    def remote(src, dst, send, recv, device):
        return pltpu.make_async_remote_copy(
            src_ref=src,
            dst_ref=dst,
            send_sem=send,
            recv_sem=recv,
            device_id=device,
            device_id_type=MESH,
        )

    barrier = pltpu.get_barrier_semaphore()
    for d in range(2):

        @pl.when(to_exists[d])
        def _():
            pl.semaphore_signal(barrier, inc=1, device_id={"exp": target[d]}, device_id_type=MESH)

    for o in range(1, X):
        pl.semaphore_signal(barrier, inc=1, device_id={"patch": column(o)}, device_id_type=MESH)
    for o in range(1, B):
        pl.semaphore_signal(barrier, inc=1, device_id={"band": other_band(o)}, device_id_type=MESH)

    H = S // 2
    win = (win0, win1)
    gs = max(owned // 2, 1)
    groups = owned // gs
    bounds = ((0, H - 16), (H - 16, S))

    def var_copy(n):
        return pltpu.make_async_copy(
            variance.at[0, n // slots, lax.rem(n, slots)], inv.at[n], var_sem.at[n]
        )

    def exp_copy(n):
        return pltpu.make_async_copy(
            exposures.at[0, n // slots, lax.rem(n, slots)], expo.at[n], exp_sem.at[n]
        )

    def own_copy(h):
        return pltpu.make_async_copy(
            templates.at[0, :, pl.ds(h * H, H)],
            win[h].at[pl.ds(row_patches + x * owned, owned)],
            local_sem.at[h],
        )

    def start_local(n, carry):
        var_copy(n).start()
        return carry

    lax.fori_loop(0, N, start_local, 0)
    pl.semaphore_wait(
        barrier,
        (z > 0).astype(jnp.int32) + (z < Z - 1).astype(jnp.int32) + (X - 1) + (B - 1),
    )

    def block(h, i):
        return templates.at[0, pl.ds(i * gs, gs), pl.ds(h * H, H)]

    def place(h, row, o, i):
        return win[h].at[pl.ds(row * row_patches + column(o) * owned + i * gs, gs)]

    def x_copy(h, o, i):
        return remote(
            block(h, i),
            place(h, 1, 0, i),
            xs_sem.at[h, o, i],
            xr_sem.at[h, o, i],
            {"patch": back_column(o)},
        )

    def z_copy(h, d, o, i):
        return remote(
            block(h, i) if o == 0 else place(h, 1, o, i),
            place(h, lands[d], o, i),
            zs_sem.at[h, d, o, i],
            zr_sem.at[h, d, o, i],
            {"exp": target[d]},
        )

    def launch_x(h):
        for i in range(groups):
            for o in range(1, X):
                x_copy(h, o, i).start()

    def launch_z(h):
        for i in range(groups):
            for d in range(2):

                @pl.when(to_exists[d])
                def _():
                    z_copy(h, d, 0, i).start()

    def forward(h):
        for i in range(groups):
            for o in range(1, X):
                x_copy(h, o, i).wait_recv()
                for d in range(2):

                    @pl.when(to_exists[d])
                    def _():
                        z_copy(h, d, o, i).start()

    def half_copy(buffer, send, recv, o, n):
        return remote(
            buffer.at[n, :, 0:C],
            buffer.at[n, :, o * C : (o + 1) * C],
            send.at[o, n],
            recv.at[o, n],
            {"band": back_band(o)},
        )

    def invert(n, carry):
        var_copy(n).wait()
        weight = 1.0 / inv[n]
        inv[n] = weight
        ifull[n, :, 0:C] = weight.astype(jnp.bfloat16)
        for o in range(1, B):
            half_copy(ifull, is_sem, ir_sem, o, n).start()
        return carry

    launch_x(0)
    launch_z(0)
    launch_x(1)

    def start_exposure(n, carry):
        exp_copy(n).start()
        return carry

    lax.fori_loop(0, N, start_exposure, 0)
    for h in range(2):
        own_copy(h).start()
    lax.fori_loop(0, N // 2, invert, 0)
    forward(0)
    launch_z(1)
    lax.fori_loop(N // 2, N, invert, 0)

    count = len(profiles)
    gcat[...] = jnp.zeros((S, 2 * count * H), jnp.bfloat16)
    for p, table in enumerate(profile_tables(-offsets(H, H, 0))):
        table = table.astype(jnp.bfloat16)
        gcat[0:H, p * H : (p + 1) * H] = table
        gcat[H:S, (count + p) * H : (count + p + 1) * H] = table
    for p, table in enumerate(profile_tables(-offsets(16, H, -H))):
        gcat[H : H + 16, p * H : (p + 1) * H] = table.astype(jnp.bfloat16)
    for p, table in enumerate(profile_tables(-offsets(16, H, 16))):
        gcat[H - 16 : H, (count + p) * H : (count + p + 1) * H] = table.astype(jnp.bfloat16)
    shifts = [(b - other_band(o)) * C for o in range(B)]
    for p, table in enumerate(profile_tables(offsets(C, C, 0))):
        gtab[p, 0:C, :] = table
    for o in range(1, B):
        start = C + (o - 1) * 32
        for p, table in enumerate(profile_tables(offsets(16, C, shifts[o]))):
            gtab[p, start : start + 16, :] = table
        for p, table in enumerate(profile_tables(offsets(16, C, shifts[o] - C + 16))):
            gtab[p, start + 16 : start + 32, :] = table

    def mix(n, carry):
        e, k = n // slots, lax.rem(n, slots)
        if B > 1:
            mats[n, C : B * C, :] = jnp.zeros(((B - 1) * C, count * C), jnp.bfloat16)
        index = 0
        for p, (group, power) in enumerate(profiles):
            value = coeff[0, e, k, index] * gtab[starts[group]]
            index += 1
            for j in range(1, degrees[group] + 1 - power):
                value = value + coeff[0, e, k, index] * gtab[starts[group] + j]
                index += 1
            value = value.astype(jnp.bfloat16)
            lanes = slice(p * C, (p + 1) * C)
            mats[n, 0:C, lanes] = value[0:C]
            for o in range(1, B):
                start = C + (o - 1) * 32
                mats[n, o * C : o * C + 16, lanes] = value[start : start + 16]
                mats[n, (o + 1) * C - 16 : (o + 1) * C, lanes] = value[start + 16 : start + 32]
        return carry

    forward(1)
    lax.fori_loop(0, N, mix, 0)

    for d in range(2):

        @pl.when(jnp.logical_not(from_exists[d]))
        def _():
            for h in range(2):

                def clear(i, carry):
                    win[h][lands[d] * row_patches + i] = jnp.zeros((H, C), jnp.bfloat16)
                    return carry

                lax.fori_loop(0, row_patches, clear, 0)

    def spread(n, carry):
        e, k = n // slots, lax.rem(n, slots)

        def put(low, square, rows, lanes, table):
            low[n, rows, lanes] = table.astype(jnp.bfloat16)
            square[n, rows, lanes] = (table * table).astype(jnp.bfloat16)

        width = jnp.full((1, H), psf[0, e, 0, k], jnp.float32)
        prow[n] = jnp.zeros((S, S), jnp.bfloat16)
        qrow[n] = jnp.zeros((S, S), jnp.bfloat16)
        table = point_table(offsets(H, H, 0), width)
        put(prow, qrow, slice(0, H), slice(0, H), table)
        put(prow, qrow, slice(H, S), slice(H, S), table)
        put(prow, qrow, slice(H, H + 16), slice(0, H), point_table(offsets(16, H, -H), width))
        put(prow, qrow, slice(H - 16, H), slice(H, S), point_table(offsets(16, H, 16), width))
        width = jnp.full((1, C), psf[0, e, 1, k], jnp.float32)
        pcol[n] = jnp.zeros((B * C, C), jnp.bfloat16)
        qcol[n] = jnp.zeros((B * C, C), jnp.bfloat16)
        lanes = slice(0, C)
        put(pcol, qcol, slice(0, C), lanes, point_table(offsets(C, C, 0), width))
        for o in range(1, B):
            first, last = o * C, (o + 1) * C
            table = point_table(offsets(16, C, shifts[o]), width)
            put(pcol, qcol, slice(first, first + 16), lanes, table)
            table = point_table(offsets(16, C, shifts[o] - C + 16), width)
            put(pcol, qcol, slice(last - 16, last), lanes, table)
        return carry

    def alive_of(n):
        e, k = n // slots, lax.rem(n, slots)
        return jnp.where(k < live[0, e], 1.0, 0.0).astype(jnp.float32)

    def matched(chains):
        middle = [
            jnp.dot(rows, full, preferred_element_type=jnp.float32).astype(jnp.bfloat16)
            for rows, full, _ in chains
        ]
        return [
            jnp.dot(part, chain[2], preferred_element_type=jnp.float32)
            for part, chain in zip(middle, chains)
        ]

    def denominator(step, carry):
        tiles = [step * 4 + a for a in range(4)]
        for n in tiles:
            for o in range(1, B):
                half_copy(ifull, is_sem, ir_sem, o, n).wait_recv()
        results = matched([(qrow[n], ifull[n], qcol[n]) for n in tiles])
        for n, result in zip(tiles, results):
            rden[n] = lax.rsqrt(result) * alive_of(n)
        return carry

    def arrive(h):
        own_copy(h).wait()
        for d in range(2):

            @pl.when(from_exists[d])
            def _():
                for o in range(X):
                    for i in range(groups):
                        z_copy(h, d, o, i).wait_recv()

    def tile_copy(h, o, n):
        return remote(
            tfull.at[h, n, :, 0:C],
            tfull.at[h, n, :, o * C : (o + 1) * C],
            ts_sem.at[h, o, n],
            tr_sem.at[h, o, n],
            {"band": back_band(o)},
        )

    def middle(h):
        first, last = bounds[h]
        depth = (h + 1) * count * H

        def choose(n, carry):
            tfull[h, n, :, 0:C] = win[h][ids[0, n // slots, lax.rem(n, slots)]]
            for o in range(1, B):
                tile_copy(h, o, n).start()
            return carry

        for n in range(N):
            choose(n, 0)
        for n in range(N):
            if h == 0:
                exp_copy(n).wait()
            for o in range(1, B):
                tile_copy(h, o, n).wait_recv()
            tile = tfull[h, n]
            pair, a = n // 2, n % 2
            for p in range(0, count, 2):
                wide = min(2, count - p)
                part = jnp.dot(
                    tile,
                    mats[n, :, p * C : (p + wide) * C],
                    preferred_element_type=jnp.float32,
                ).astype(jnp.bfloat16)
                for v in range(wide):
                    row = (h * count + p + v) * H
                    cols[pair, row : row + H, a * C : (a + 1) * C] = part[:, v * C : (v + 1) * C]
        for pair in range(N // 2):
            convolved = jnp.dot(
                gcat[first:last, 0:depth],
                cols[pair, 0:depth, :],
                preferred_element_type=jnp.float32,
            )
            for a in range(2):
                n = pair * 2 + a
                value = expo[n, first:last, :].astype(jnp.float32)
                value = (value - convolved[:, a * C : (a + 1) * C]) * inv[n, first:last, :]
                wval[n, first:last, :] = value
                wfull[n, first:last, 0:C] = value.astype(jnp.bfloat16)
                if h == 1:
                    for o in range(1, B):
                        half_copy(wfull, ws_sem, wr_sem, o, n).start()

    def partials(h, q, rows):
        first, last = bounds[h]
        factors = []
        for row in rows:
            hits = []
            for n in range(N):
                e, k = n // slots, n % slots
                hit = jnp.logical_and(ids[0, e, k] == row * row_patches + q, k < live[0, e])
                hits.append(jnp.where(hit, 1.0, 0.0).astype(jnp.float32))
            factors.append(hits)
        step = 16
        for start in range(first, last, step):
            values = [jnp.zeros((step, C), jnp.float32) for _ in rows]
            for n in range(N):
                tile = wval[n, start : start + step, :]
                values = [value + hits[n] * tile for value, hits in zip(values, factors)]
            yield slice(start, start + step), values

    def p_copy(h, d, q, t):
        first, last = bounds[h]
        rows = pl.ds(first, last - first)
        return remote(
            psend.at[d, q, rows],
            precv.at[d, q, rows],
            ps_sem.at[h, d, t],
            pr_sem.at[h, d, t],
            {"exp": target[d]},
        )

    def patch_of(t):
        return lax.rem(x + 1 + t // owned, X) * owned + lax.rem(t, owned)

    def push(h):
        def step(t, carry):
            q = patch_of(t)
            for rows, (up, own, down) in partials(h, q, (0, 1, 2)):
                psend[0, q, rows, :] = up.astype(jnp.bfloat16)
                psend[1, q, rows, :] = down.astype(jnp.bfloat16)
                pown[q, rows, :] = own
            for d in range(2):

                @pl.when(to_exists[d])
                def _():
                    p_copy(h, d, q, t).start()

            return carry

        lax.fori_loop(0, row_patches, step, 0)

    def numerator(step, carry):
        tiles = [step * 4 + a for a in range(4)]
        for n in tiles:
            for o in range(1, B):
                half_copy(wfull, ws_sem, wr_sem, o, n).wait_recv()
        results = matched([(prow[n], wfull[n], pcol[n]) for n in tiles])
        for n, result in zip(tiles, results):
            score[0, n // slots, lax.rem(n, slots)] = result * rden[n]
        return carry

    def gather_rows(h, t, q):
        first, last = bounds[h]
        for d in range(2):

            @pl.when(from_exists[d])
            def _():
                p_copy(h, d, q, t).wait_recv()
                pown[q, first:last, :] += precv[d, q, first:last, :].astype(jnp.float32)

    def s_copy(h, s, i):
        first, last = bounds[h]
        rows = pl.ds(first, last - first)
        return remote(
            xsend.at[s, i, rows],
            xrecv.at[s, i, rows],
            ss_sem.at[h, s, i],
            sr_sem.at[h, s, i],
            {"patch": column(s + 1)},
        )

    def pass_on(h):
        first, last = bounds[h]
        for s in range(X - 1):
            for i in range(owned):
                q = column(s + 1) * owned + i
                gather_rows(h, s * owned + i, q)
                xsend[s, i, first:last, :] = pown[q, first:last, :].astype(jnp.bfloat16)
                s_copy(h, s, i).start()

    def finish_sums(h):
        first, last = bounds[h]
        for i in range(owned):
            q = x * owned + i
            gather_rows(h, (X - 1) * owned + i, q)
            value = pown[q, first:last, :]
            for s in range(X - 1):
                s_copy(h, s, i).wait_recv()
                value = value + xrecv[s, i, first:last, :].astype(jnp.float32)
            coadd[0, i, first:last, :] = value

    arrive(0)
    middle(0)
    push(0)
    lax.fori_loop(0, N, spread, 0)
    denominator(0, 0)
    arrive(1)
    middle(1)
    push(1)
    pass_on(0)
    lax.fori_loop(1, N // 4, denominator, 0)
    pass_on(1)
    finish_sums(0)
    lax.fori_loop(0, N // 4, numerator, 0)
    finish_sums(1)

    for h in range(2):
        for o in range(1, X):
            for i in range(groups):
                x_copy(h, o, i).wait_send()
            for i in range(owned):
                s_copy(h, o - 1, i).wait_send()
        for d in range(2):

            @pl.when(to_exists[d])
            def _():
                for o in range(X):
                    for i in range(groups):
                        z_copy(h, d, o, i).wait_send()

                def sent(t, carry):
                    p_copy(h, d, patch_of(t), t).wait_send()
                    return carry

                lax.fori_loop(0, row_patches, sent, 0)

    def finish(n, carry):
        for o in range(1, B):
            half_copy(ifull, is_sem, ir_sem, o, n).wait_send()
            half_copy(wfull, ws_sem, wr_sem, o, n).wait_send()
            for h in range(2):
                tile_copy(h, o, n).wait_send()
        return carry

    lax.fori_loop(0, N, finish, 0)


def on_device(templates, exposures, variance, coefficients, psf_width, patch_ids, live_count):
    owned, S, C = templates.shape[1:]
    Z, X, B = (lax.axis_size(axis) for axis in ("exp", "patch", "band"))
    N = patch_ids.shape[1] * patch_ids.shape[2]
    row = X * owned
    count = len(profiles)
    bf16, f32 = jnp.bfloat16, jnp.float32
    dma = pltpu.SemaphoreType.DMA
    scratch = [
        pltpu.VMEM((3 * row, S // 2, C), bf16),
        pltpu.VMEM((3 * row, S // 2, C), bf16),
        pltpu.VMEM((2, N, S // 2, B * C), bf16),
        pltpu.VMEM((N, B * C, count * C), bf16),
        pltpu.VMEM((S, count * S), bf16),
        pltpu.VMEM((count, C + 32 * (B - 1), C), f32),
        pltpu.VMEM((N // 2, count * S, 2 * C), bf16),
        pltpu.VMEM((N, S, C), bf16),
        pltpu.VMEM((N, S, C), f32),
        pltpu.VMEM((N, S, C), f32),
        pltpu.VMEM((N, S, B * C), bf16),
        pltpu.VMEM((N, S, B * C), bf16),
        pltpu.VMEM((N, S, C), f32),
        pltpu.VMEM((N, S, S), bf16),
        pltpu.VMEM((N, S, S), bf16),
        pltpu.VMEM((N, B * C, C), bf16),
        pltpu.VMEM((N, B * C, C), bf16),
        pltpu.VMEM((2, row, S, C), bf16),
        pltpu.VMEM((2, row, S, C), bf16),
        pltpu.VMEM((row, S, C), f32),
        pltpu.VMEM((max(X - 1, 1), owned, S, C), bf16),
        pltpu.VMEM((max(X - 1, 1), owned, S, C), bf16),
        dma((2,)),
        dma((N,)),
        dma((N,)),
        dma((2, X, owned)),
        dma((2, X, owned)),
        dma((2, 2, X, owned)),
        dma((2, 2, X, owned)),
        dma((2, B, N)),
        dma((2, B, N)),
        dma((B, N)),
        dma((B, N)),
        dma((B, N)),
        dma((B, N)),
        dma((2, 2, row)),
        dma((2, 2, row)),
        dma((2, max(X - 1, 1), owned)),
        dma((2, max(X - 1, 1), owned)),
    ]
    any_spec = pl.BlockSpec(memory_space=pl.ANY)
    vmem = pl.BlockSpec(memory_space=pltpu.VMEM)
    smem = pl.BlockSpec(memory_space=pltpu.SMEM)
    return pl.pallas_call(
        functools.partial(kernel, (Z, X, B)),
        out_shape=(
            pltpu.VMEM(templates.shape, f32),
            pltpu.VMEM(exposures.shape, f32),
        ),
        in_specs=[any_spec] * 3 + [smem] * 4,
        out_specs=(vmem, vmem),
        scratch_shapes=scratch,
        compiler_params=pltpu.CompilerParams(
            collective_id=0, has_side_effects=True, vmem_limit_bytes=56 * 2**20
        ),
    )(
        templates,
        exposures,
        variance,
        coefficients,
        jnp.swapaxes(psf_width, 2, 3),
        patch_ids,
        live_count,
    )


def solution(mesh):
    in_specs = (
        P(("groups", "exp"), "patch", None, "band"),
        P(("groups", "exp"), "patch", None, None, "band"),
        P(("groups", "exp"), "patch", None, None, "band"),
        P(("groups", "exp"), "patch", None, None),
        P(("groups", "exp"), "patch", None, None),
        P(("groups", "exp"), "patch", None),
        P(("groups", "exp"), "patch"),
    )
    out_specs = (
        P(("groups", "exp"), "patch", None, "band"),
        P(("groups", "exp"), "patch", None, None, "band"),
    )
    return jax.shard_map(
        on_device, mesh=mesh, in_specs=in_specs, out_specs=out_specs, check_vma=False
    )
```
